256 devices in a mesh: group: 16 (over x, z_lo, core), seq: 16 (over y, z_hi).
Axes of the slice: x: 4, y: 4, z: 8 (z_hi: 4, z_lo: 2; z = z_hi * 2 + z_lo), core: 2. Of those that a mesh axis runs over, the one named last changes fastest.
Arguments:
- step_inputs: bfloat16 [4, 64, 8192], P(None, 'group', 'seq'), may hold values from -6 to 6
- norm_gain: bfloat16 [8192], P('seq'), may hold values from 0.5 to 2
- w_query: bfloat16 [8192, 4096], P('seq'), may hold values from -0.0625 to 0.0625
- w_keyval: bfloat16 [8192, 1024], P('seq'), may hold values from -0.0625 to 0.0625
- w_out: bfloat16 [4096, 8192], P('seq'), may hold values from -0.25 to 0.25
- key_cache: bfloat16 [64, 512, 512], P('group', 'seq'), may hold values from -420 to 420
- value_cache: bfloat16 [64, 512, 512], P('group', 'seq'), may hold values from -6 to 6
- ctx_len: int32 [64], P('group'), may hold values from 2 to 512, as said below
- mig_slot: int32 [4, 16], replicated, may hold values from 0 to 3
- mig_shift: int32 [4], replicated, may hold values from 1 to 15, as said below
Outputs:
- attn_output: bfloat16 [4, 64, 8192], P(None, 'group', 'seq')
The draws below stay inside these ranges and needn't reach their ends.
Inputs may be any that keep to these rules, and one draw needn't show every extreme that they name: `ctx_len`: at least two cached positions per slot; some slot holds all 512. Group g sends to group (g + mig_shift[s]) mod 16.
All inputs are finite; a program needn't handle non-finite values.
Results may differ from the reference program's by a relative error of at most 0.034.
Values may be sent and summed in bfloat16 or wider, within the bound.
No kernel may reach another device: no remote copies, remote signals or barrier semaphores. Data moves between devices by JAX's collectives and lax.ppermute only.
A program may use at most 128 MiB of HBM per device.

```python
import math
from functools import partial
import jax
import jax.numpy as jnp
from jax import lax

D = 8192
H = 32
KVH = 4
HD = 128
STEPS = 4
REQ = 4
GROUPS = 16
ROWS = 64
CONTEXT = 512


def draw_key_cache(key, part):
    key = jax.random.fold_in(key, 11)
    base_key = jax.random.fold_in(key, 0)
    shape = (ROWS, CONTEXT, KVH * HD)
    keys_all = jnp.clip(2.0 * jax.random.normal(base_key, shape, jnp.float32), -12.0, 12.0)
    return keys_all.astype(jnp.bfloat16)


def draw_ctx_len(key, part):
    key = jax.random.fold_in(key, 12)
    lengths = jax.random.randint(key, (ROWS,), 2, CONTEXT + 1, jnp.int32)
    return lengths.at[0].set(CONTEXT)


def draw_mig_shift(key, part):
    key = jax.random.fold_in(key, 13)
    shifts = jax.random.randint(key, (STEPS,), 1, GROUPS, jnp.int32)
    return shifts.at[0].set(GROUPS - 1)


def set_ends(values, rng, low, high):
    longest = values.shape.index(max(values.shape))
    spots = []
    for shift in (0, 1):
        where = [jax.random.randint(jax.random.fold_in(rng, axis), (), 0, length) for axis, length in enumerate(values.shape)]
        where[longest] = (where[longest] + shift) % values.shape[longest]
        spots.append(tuple(where))
    return values.at[spots[0]].set(low).at[spots[1]].set(high)


def steps_of(key, extent, cuts, smallest, largest):
    gain = 1.0
    for axis_at, parts in cuts:
        heights = jax.random.uniform(jax.random.fold_in(jax.random.fold_in(key, 6), axis_at), (parts,), jnp.float32, smallest / len(cuts), largest / len(cuts))
        gain = gain * jnp.repeat(jnp.exp(heights), extent[axis_at] // parts).reshape((-1,) + (1,) * (len(extent) - 1 - axis_at))
    return gain


def scatter_about(own_key, shape, spread, bound, cuts=(), held_as=jnp.bfloat16):
    values = spread * jax.random.normal(own_key, shape, jnp.float32)
    if cuts:
        values = values * steps_of(own_key, shape, cuts, -0.22, 0.18)
    return jnp.clip(values, -bound, bound).astype(held_as)


def setup_inputs(seed: int = 0) -> dict:
    key_list = jax.random.split(jax.random.key(seed), 11)
    step_inputs = scatter_about(key_list[0], (STEPS, ROWS, D), 1.0, 6.0, ((1, 16), (2, 16)))
    norm_gain = jnp.clip(jnp.exp(math.log(2.0) - 1.3862944 * jax.random.uniform(key_list[1], (D,), jnp.float32) ** steps_of(key_list[1], (D,), ((0, 16),), -0.2, 0.2)), 0.5, 2.0).astype(jnp.bfloat16)
    w_query = scatter_about(key_list[2], (D, H * HD), D ** -0.5, 0.0625, ((0, 16),))
    w_keyval = scatter_about(key_list[3], (D, 2 * KVH * HD), D ** -0.5, 0.0625, ((0, 16),))
    w_out = scatter_about(key_list[4], (H * HD, D), (KVH * HD) ** -0.5, 0.25, ((0, 16),))
    key_cache = draw_key_cache(jax.random.fold_in(key_list[10], 71), 0)
    value_cache = scatter_about(key_list[6], (ROWS, CONTEXT, KVH * HD), 1.0, 6.0, ((0, 16), (1, 16)))
    ctx_len = draw_ctx_len(jax.random.fold_in(key_list[10], 71), 0)
    mig_slot = set_ends(jax.random.randint(key_list[8], (STEPS, GROUPS), 0, REQ), jax.random.fold_in(key_list[8], 1), 0, REQ - 1).astype(jnp.int32)
    mig_shift = draw_mig_shift(jax.random.fold_in(key_list[10], 71), 0)
    return dict(step_inputs=step_inputs, norm_gain=norm_gain, w_query=w_query, w_keyval=w_keyval, w_out=w_out, key_cache=key_cache, value_cache=value_cache, ctx_len=ctx_len, mig_slot=mig_slot, mig_shift=mig_shift)


norm_eps = 1e-06
rope_base = 1000000.0

def rotary(values, position):
    half = values.shape[-1] // 2
    exponent = jnp.arange(half, dtype=jnp.float32) * (2.0 / values.shape[-1])
    inverse = jnp.power(jnp.float32(rope_base), -exponent)
    angles = position.astype(jnp.float32)[..., None, None] * inverse
    cosine = jnp.cos(angles)
    sine = jnp.sin(angles)
    first = values[..., :half]
    second = values[..., half:]
    return jnp.concatenate([first * cosine - second * sine, second * cosine + first * sine], axis=-1)

def attend_group(packed, step):
    queries, keys, values, recent_keys, recent_values, lengths = packed
    per_kv = H // KVH
    scale = 1.0 / jnp.sqrt(jnp.float32(HD))
    query_f = queries.astype(jnp.float32).reshape(REQ, KVH, per_kv, HD)
    cache_f = keys.astype(jnp.float32).reshape(REQ, CONTEXT, KVH, HD)
    recent_f = recent_keys.astype(jnp.float32).reshape(REQ, STEPS, KVH, HD)
    scores = jnp.einsum('rkgd,rckd->rkgc', query_f, cache_f) * scale
    recent_scores = jnp.einsum('rkgd,rckd->rkgc', query_f, recent_f) * scale
    live = (jnp.arange(CONTEXT, dtype=jnp.int32)[None, :] < lengths[:, None])[:, None, None, :]
    recent_live = (jnp.arange(STEPS, dtype=jnp.int32) <= step)[None, None, None, :]
    neg = jnp.float32(-jnp.inf)
    every = jnp.concatenate([jnp.where(live, scores, neg), jnp.where(recent_live, recent_scores, neg)], axis=-1)
    top = lax.optimization_barrier(jnp.max(every, axis=-1, keepdims=True))
    weights = jnp.exp(every - top)
    total = lax.optimization_barrier(jnp.sum(weights, axis=-1))
    rounded = lax.optimization_barrier(weights.astype(jnp.bfloat16)).astype(jnp.float32)
    all_values = jnp.concatenate([values, recent_values], axis=1).astype(jnp.float32)
    all_values = all_values.reshape(REQ, CONTEXT + STEPS, KVH, HD)
    summed = jnp.einsum('rkgc,rckd->rkgd', rounded, all_values)
    result = summed / total[..., None]
    return result.reshape(REQ, H * HD).astype(jnp.bfloat16)

def reference(step_inputs, norm_gain, w_query, w_keyval, w_out, key_cache, value_cache, ctx_len, mig_slot, mig_shift):
    kv_width = KVH * HD
    keys = key_cache.reshape(GROUPS, REQ, CONTEXT, kv_width)
    values = value_cache.reshape(GROUPS, REQ, CONTEXT, kv_width)
    lengths = ctx_len.reshape(GROUPS, REQ)
    recent_keys = jnp.zeros((GROUPS, REQ, STEPS, kv_width), jnp.bfloat16)
    recent_values = jnp.zeros((GROUPS, REQ, STEPS, kv_width), jnp.bfloat16)
    group_ids = jnp.arange(GROUPS, dtype=jnp.int32)
    results = []
    for step in range(STEPS):
        slots = mig_slot[step]
        source = ((group_ids - mig_shift[step]) % GROUPS).astype(jnp.int32)
        source_slot = slots[source]
        keys = keys.at[group_ids, slots].set(keys[source, source_slot])
        values = values.at[group_ids, slots].set(values[source, source_slot])
        lengths = lengths.at[group_ids, slots].set(lengths[source, source_slot])
        recent_keys = recent_keys.at[group_ids, slots].set(recent_keys[source, source_slot])
        recent_values = recent_values.at[group_ids, slots].set(recent_values[source, source_slot])
        inputs = step_inputs[step].astype(jnp.float32)
        inverse = lax.rsqrt(lax.optimization_barrier(jnp.mean(inputs * inputs, axis=-1)) + norm_eps)
        normed = (inputs * norm_gain.astype(jnp.float32)).astype(jnp.bfloat16)
        query = jnp.dot(normed, w_query, preferred_element_type=jnp.float32) * inverse[:, None]
        keyval = jnp.dot(normed, w_keyval, preferred_element_type=jnp.float32) * inverse[:, None]
        position = lengths.reshape(ROWS) + step
        query = rotary(query.reshape(ROWS, H, HD), position).astype(jnp.bfloat16)
        new_key = rotary(keyval[:, :kv_width].reshape(ROWS, KVH, HD), position).reshape(ROWS, kv_width).astype(jnp.bfloat16)
        new_value = keyval[:, kv_width:].astype(jnp.bfloat16)
        recent_keys = recent_keys.at[:, :, step].set(new_key.reshape(GROUPS, REQ, kv_width))
        recent_values = recent_values.at[:, :, step].set(new_value.reshape(GROUPS, REQ, kv_width))
        attended = lax.map(partial(attend_group, step=step), (query.reshape(GROUPS, REQ, H, HD), keys, values, recent_keys, recent_values, lengths))
        projected = jnp.dot(attended.reshape(ROWS, H * HD), w_out, preferred_element_type=jnp.float32)
        results.append(projected.astype(jnp.bfloat16))
    return jnp.stack(results)
```

```python
import functools

import jax
import jax.numpy as jnp
import numpy as np
from jax import lax
from jax.experimental import pallas as pl
from jax.experimental.pallas import tpu as pltpu
from jax.sharding import Mesh
from jax.sharding import PartitionSpec as P

D = 8192
H = 32
KVH = 4
HD = 128
STEPS = 4
REQ = 4
GROUPS = 16
SEQ = 16
PER_KV = H // KVH
LOCAL = 32
CONTEXT = SEQ * LOCAL
KV_WIDTH = KVH * HD
ROWS = STEPS * REQ
CHUNK = 2 * LOCAL + PER_KV * STEPS + 16

norm_eps = 1e-06
rope_base = 1000000.0
masked_score = -1e30

f32 = jnp.float32
bf16 = jnp.bfloat16


def full(shape):
    return pl.BlockSpec(shape, lambda *_: (0,) * len(shape))


def smem():
    return pl.BlockSpec(memory_space=pltpu.SMEM)


def params():
    return pltpu.CompilerParams(
        dimension_semantics=("arbitrary",), vmem_limit_bytes=48 * 1024 * 1024
    )


def wrap(value):
    return jnp.where(value >= GROUPS, value - GROUPS, value)


def project_kernel(
    slot_ref,
    shift_ref,
    group_ref,
    x_ref,
    gain_ref,
    wq_ref,
    wk_ref,
    wv_ref,
    kc_ref,
    vc_ref,
    out_ref,
    normed_ref,
    squares_ref,
):
    row8 = lax.broadcasted_iota(jnp.int32, (8, HD), 0)
    lane = lax.broadcasted_iota(jnp.int32, (8, HD), 1)

    @pl.when(pl.program_id(0) == 0)
    def _():
        tiles = []
        for r in range(REQ):
            at_group = group_ref[0]
            at_slot = jnp.int32(r)
            tile = jnp.zeros((8, HD), jnp.int32)
            for s in range(STEPS):
                leaves = slot_ref[s, at_group] == at_slot
                next_group = wrap(at_group + shift_ref[s])
                next_slot = slot_ref[s, next_group]
                at_group = jnp.where(leaves, next_group, at_group)
                at_slot = jnp.where(leaves, next_slot, at_slot)
                column = at_group * ROWS + s * REQ + at_slot
                tile = jnp.where((row8 & 3) == s, column, tile)
            tiles.append(tile)
        target = jnp.concatenate(tiles, axis=0)
        lanes = lax.broadcasted_iota(jnp.int32, (8 * REQ, HD), 1)
        x = jnp.zeros((8 * REQ, x_ref.shape[1]), f32)
        for part in range(GROUPS * ROWS // HD):
            pick = jnp.where(target == lanes + part * HD, 1.0, 0.0).astype(bf16)
            x = x + jnp.dot(
                pick, x_ref[part * HD : (part + 1) * HD, :], preferred_element_type=f32
            )
        squares_ref[...] = jnp.broadcast_to(
            jnp.sum(x * x, axis=-1, keepdims=True), squares_ref.shape
        )
        normed_ref[...] = (x * gain_ref[...].astype(f32)).astype(bf16)

    normed = normed_ref[...]
    query = jnp.dot(normed, wq_ref[...], preferred_element_type=f32)
    key = jnp.dot(normed, wk_ref[...], preferred_element_type=f32)
    value = jnp.dot(normed, wv_ref[...], preferred_element_type=f32)
    squares = squares_ref[...]
    high = squares.astype(bf16).astype(f32)
    squares = jnp.where(lax.broadcasted_iota(jnp.int32, squares.shape, 1) < HD // 2, high, squares - high)
    for r in range(REQ):
        rows = slice(r * 8, r * 8 + 8)
        tiles = [
            jnp.where(
                row8 < 4,
                query[rows, 2 * i * HD : (2 * i + 1) * HD],
                query[rows, (2 * i + 1) * HD : (2 * i + 2) * HD],
            )
            for i in range(PER_KV // 2)
        ]
        tiles.append(jnp.where(row8 < 4, key[rows], value[rows]))
        tiles.append(squares[rows])
        out_ref[r, 0:LOCAL, :] = kc_ref[r]
        out_ref[r, LOCAL : 2 * LOCAL, :] = vc_ref[r]
        out_ref[r, 2 * LOCAL : CHUNK, :] = jnp.concatenate(tiles, axis=0).astype(bf16)


def attend_kernel(len_ref, own_ref, freq_ref, in_ref, out_ref):
    length = len_ref[own_ref[0]]
    row8 = lax.broadcasted_iota(jnp.int32, (8, HD), 0)
    lane = lax.broadcasted_iota(jnp.int32, (8, HD), 1)
    total = in_ref[0, 2 * LOCAL : CHUNK, :].astype(f32)
    for k in range(1, SEQ):
        total = total + in_ref[k, 2 * LOCAL : CHUNK, :].astype(f32)
    squares = jnp.sum(total[40:48], axis=-1, keepdims=True) * (2.0 / HD)
    inverse = lax.rsqrt(squares / D + norm_eps)
    position = (length + (row8 & 3)).astype(f32)
    angles = position * freq_ref[...]
    cosine = jnp.cos(angles)
    sine = jnp.where(lane < HD // 2, -jnp.sin(angles), jnp.sin(angles))

    def rotated(tile):
        return tile * cosine + pltpu.roll(tile, HD // 2, 1) * sine

    query = jnp.concatenate(
        [rotated(total[i * 8 : i * 8 + 8] * inverse) for i in range(4)], axis=0
    ).astype(bf16)
    fresh = total[32:40] * inverse
    new_key = rotated(fresh)
    new_value = pltpu.roll(fresh, 4, 0)
    empty = jnp.zeros((HD - 8, HD), f32)
    new_key = jnp.concatenate([new_key, empty], axis=0).astype(bf16)
    new_value = jnp.concatenate([new_value, empty], axis=0).astype(bf16)

    keys = in_ref[:, 0:LOCAL, :].reshape(CONTEXT, HD)
    values = in_ref[:, LOCAL : 2 * LOCAL, :].reshape(CONTEXT, HD)
    scale = 1.0 / np.sqrt(np.float32(HD))
    contract = (((1,), (1,)), ((), ()))
    scores = lax.dot_general(query, keys, contract, preferred_element_type=f32) * scale
    recent = lax.dot_general(query, new_key, contract, preferred_element_type=f32) * scale
    column = lax.broadcasted_iota(jnp.int32, scores.shape, 1)
    scores = jnp.where(column < length, scores, masked_score)
    step = lax.broadcasted_iota(jnp.int32, recent.shape, 0) & 3
    recent = jnp.where(
        lax.broadcasted_iota(jnp.int32, recent.shape, 1) <= step, recent, masked_score
    )
    peak = jnp.maximum(
        jnp.max(scores, axis=-1, keepdims=True), jnp.max(recent, axis=-1, keepdims=True)
    )
    weights = jnp.exp(scores - peak)
    recent_weights = jnp.exp(recent - peak)
    count = jnp.sum(weights, axis=-1, keepdims=True) + jnp.sum(
        recent_weights, axis=-1, keepdims=True
    )
    summed = jnp.dot(weights.astype(bf16), values, preferred_element_type=f32) + jnp.dot(
        recent_weights.astype(bf16), new_value, preferred_element_type=f32
    )
    attention = (summed / count).astype(bf16)
    rows = attention.shape[0]
    for g in range(GROUPS):
        out_ref[g * rows : (g + 1) * rows, :] = attention


def output_kernel(slot_ref, shift_ref, group_ref, in_ref, w_ref, out_ref, attention_ref):
    @pl.when(pl.program_id(0) == 0)
    def _():
        row = lax.broadcasted_iota(jnp.int32, (2 * ROWS, HD), 0)
        lane = lax.broadcasted_iota(jnp.int32, (2 * ROWS, HD), 1)
        target = jnp.zeros((2 * ROWS, HD), jnp.int32)
        for s in range(STEPS):
            for r in range(REQ):
                at_group = group_ref[0]
                at_slot = jnp.int32(r)
                for back in range(s, -1, -1):
                    came = slot_ref[back, at_group] == at_slot
                    source = wrap(at_group - shift_ref[back] + GROUPS)
                    source_slot = slot_ref[back, source]
                    at_group = jnp.where(came, source, at_group)
                    at_slot = jnp.where(came, source_slot, at_slot)
                column = (at_group * REQ + at_slot) * 8 + s
                target = jnp.where((row & (ROWS - 1)) == s * REQ + r, column, target)
        target = target + jnp.where(row >= ROWS, 4, 0)
        picked = jnp.zeros((2 * ROWS, HD), f32)
        for part in range(in_ref.shape[0] // HD):
            pick = jnp.where(target == lane + part * HD, 1.0, 0.0).astype(bf16)
            picked = picked + jnp.dot(
                pick, in_ref[part * HD : (part + 1) * HD, :], preferred_element_type=f32
            )
        attention_ref[:, 0:HD] = picked[0:ROWS].astype(bf16)
        attention_ref[:, HD : 2 * HD] = picked[ROWS : 2 * ROWS].astype(bf16)

    projected = jnp.dot(attention_ref[...], w_ref[...], preferred_element_type=f32).astype(bf16)
    width = out_ref.shape[2]
    for k in range(out_ref.shape[0]):
        out_ref[k] = projected[:, k * width : (k + 1) * width]


def body(
    step_inputs,
    norm_gain,
    w_query,
    w_keyval,
    w_out,
    key_cache,
    value_cache,
    ctx_len,
    mig_slot,
    mig_shift,
):
    width = step_inputs.shape[2]
    group = lax.axis_index("group").astype(jnp.int32).reshape(1)
    own = lax.axis_index("seq_z").astype(jnp.int32).reshape(1)
    seq = ("seq_y", "seq_z")

    x = jnp.broadcast_to(step_inputs.reshape(1, ROWS, width), (GROUPS, ROWS, width))
    x = lax.all_to_all(x, "group", 0, 0, tiled=True).reshape(GROUPS * ROWS, width)
    heads = PER_KV * HD
    sent = pl.pallas_call(
        project_kernel,
        grid=(KVH,),
        in_specs=[
            smem(),
            smem(),
            smem(),
            full((GROUPS * ROWS, width)),
            full((1, width)),
            pl.BlockSpec((width, heads), lambda i: (0, i)),
            pl.BlockSpec((width, HD), lambda i: (0, i)),
            pl.BlockSpec((width, HD), lambda i: (0, KVH + i)),
            pl.BlockSpec((REQ, LOCAL, HD), lambda i: (0, 0, i)),
            pl.BlockSpec((REQ, LOCAL, HD), lambda i: (0, 0, i)),
        ],
        out_specs=pl.BlockSpec((REQ, CHUNK, HD), lambda i: (i, 0, 0)),
        out_shape=jax.ShapeDtypeStruct((SEQ, CHUNK, HD), bf16),
        scratch_shapes=[pltpu.VMEM((8 * REQ, width), bf16), pltpu.VMEM((8 * REQ, HD), f32)],
        compiler_params=params(),
        name="project",
    )(
        mig_slot,
        mig_shift,
        group,
        x,
        norm_gain.reshape(1, width),
        w_query,
        w_keyval,
        w_keyval,
        key_cache,
        value_cache,
    )
    received = lax.all_to_all(sent, seq, 0, 0, tiled=True)

    half = np.arange(HD) % (HD // 2)
    freq = jnp.asarray((rope_base ** (-2.0 * half / HD)).astype(np.float32).reshape(1, HD))
    attention = pl.pallas_call(
        attend_kernel,
        grid=(1,),
        in_specs=[smem(), smem(), full((1, HD)), full((SEQ, CHUNK, HD))],
        out_specs=full((GROUPS * PER_KV * STEPS, HD)),
        out_shape=jax.ShapeDtypeStruct((GROUPS * PER_KV * STEPS, HD), bf16),
        compiler_params=params(),
        name="attend",
    )(ctx_len, own, freq, received)
    attention = lax.all_to_all(
        attention.reshape(GROUPS * 4, 8, HD), ("group", "seq_z"), 0, 0, tiled=True
    ).reshape(GROUPS * 4 * 8, HD)

    blocks = 4
    shares = pl.pallas_call(
        output_kernel,
        grid=(blocks,),
        in_specs=[
            smem(),
            smem(),
            smem(),
            full((GROUPS * 4 * 8, HD)),
            pl.BlockSpec((2 * HD, D // blocks), lambda i: (0, i)),
        ],
        out_specs=pl.BlockSpec((SEQ // blocks, ROWS, width), lambda i: (i, 0, 0)),
        out_shape=jax.ShapeDtypeStruct((SEQ, ROWS, width), bf16),
        scratch_shapes=[pltpu.VMEM((ROWS, 2 * HD), bf16)],
        compiler_params=params(),
        name="output",
    )(mig_slot, mig_shift, group, attention, w_out)
    shares = lax.all_to_all(shares, seq, 0, 0, tiled=True)
    result = jnp.sum(shares.astype(f32), axis=0).astype(bf16)
    return result.reshape(STEPS, REQ, width)


def solution(mesh):
    split = Mesh(mesh.devices.reshape(GROUPS, 4, 4), ("group", "seq_y", "seq_z"))
    seq = ("seq_y", "seq_z")
    placed = (
        P(None, "group", seq),
        P(seq),
        P(seq, None),
        P(seq, None),
        P(seq, None),
        P("group", seq, None),
        P("group", seq, None),
        P("group"),
        P(),
        P(),
    )
    return jax.shard_map(
        body, mesh=split, in_specs=placed, out_specs=P(None, "group", seq), check_vma=False
    )
```

```python
import jax
import jax.numpy as jnp
import numpy as np
from jax import lax
from jax.experimental import pallas as pl
from jax.experimental.pallas import tpu as pltpu
from jax.sharding import Mesh
from jax.sharding import PartitionSpec as P

D = 8192
H = 32
KVH = 4
HD = 128
STEPS = 4
REQ = 4
GROUPS = 16
SEQ = 16
PER_KV = H // KVH
LOCAL = 32
CONTEXT = SEQ * LOCAL
KV_WIDTH = KVH * HD
ROWS = STEPS * REQ
CHUNK = 2 * LOCAL + PER_KV * STEPS + 16

norm_eps = 1e-06
rope_base = 1000000.0
masked_score = -1e30

f32 = jnp.float32
bf16 = jnp.bfloat16


def anywhere():
    return pl.BlockSpec(memory_space=pl.ANY)


def in_vmem():
    return pl.BlockSpec(memory_space=pltpu.VMEM)


def params(mib=16):
    return pltpu.CompilerParams(vmem_limit_bytes=mib * 1024 * 1024)


def placed(array):
    return pltpu.with_memory_space_constraint(array, pltpu.VMEM)


def left(array):
    return pltpu.with_memory_space_constraint(array, pltpu.HBM)


def wrap(value):
    return jnp.where(value >= GROUPS, value - GROUPS, value)


def spread_kernel(x_hbm, out_ref, x_ref, sem):
    copy = pltpu.make_async_copy(x_hbm, x_ref, sem)
    copy.start()
    copy.wait()
    x = jnp.concatenate([x_ref[s].astype(f32) for s in range(STEPS)], axis=0).astype(bf16)
    for g in range(GROUPS):
        out_ref[g] = x


def prepare_kernel(
    slot_hbm,
    shift_hbm,
    len_hbm,
    group_ref,
    own_ref,
    freq_hbm,
    wq_hbm,
    wkv_hbm,
    kc_hbm,
    vc_hbm,
    pick_in_ref,
    pick_out_ref,
    table_ref,
    wkv_ref,
    kc_ref,
    vc_ref,
    wq0_ref,
    slot_ref,
    shift_ref,
    len_ref,
    freq_ref,
    sems,
):
    small = [
        pltpu.make_async_copy(slot_hbm, slot_ref, sems.at[0]),
        pltpu.make_async_copy(shift_hbm, shift_ref, sems.at[1]),
        pltpu.make_async_copy(len_hbm, len_ref, sems.at[2]),
        pltpu.make_async_copy(freq_hbm, freq_ref, sems.at[7]),
    ]
    large = [
        pltpu.make_async_copy(kc_hbm, kc_ref, sems.at[3]),
        pltpu.make_async_copy(vc_hbm, vc_ref, sems.at[4]),
        pltpu.make_async_copy(wkv_hbm, wkv_ref, sems.at[5]),
    ]
    columns = pl.ds(0, wq0_ref.shape[1])
    large.append(pltpu.make_async_copy(wq_hbm.at[:, columns], wq0_ref, sems.at[6]))
    for copy in small + large:
        copy.start()
    for copy in small:
        copy.wait()
    group = group_ref[0]
    own = own_ref[0]

    row8 = lax.broadcasted_iota(jnp.int32, (8, HD), 0)
    lane = lax.broadcasted_iota(jnp.int32, (8, HD), 1)
    for r in range(REQ):
        at_group = group
        at_slot = jnp.int32(r)
        target = jnp.zeros((8, HD), jnp.int32)
        for s in range(STEPS):
            leaves = slot_ref[s, at_group] == at_slot
            next_group = wrap(at_group + shift_ref[s])
            next_slot = slot_ref[s, next_group]
            at_group = jnp.where(leaves, next_group, at_group)
            at_slot = jnp.where(leaves, next_slot, at_slot)
            column = at_group * ROWS + s * REQ + at_slot
            target = jnp.where((row8 & 3) == s, column, target)
        for part in range(GROUPS * ROWS // HD):
            pick_in_ref[r * 8 : r * 8 + 8, part * HD : (part + 1) * HD] = jnp.where(
                target == lane + part * HD, 1.0, 0.0
            )

    row = lax.broadcasted_iota(jnp.int32, (2 * ROWS, HD), 0)
    lanes = lax.broadcasted_iota(jnp.int32, (2 * ROWS, HD), 1)
    target = jnp.zeros((2 * ROWS, HD), jnp.int32)
    for s in range(STEPS):
        for r in range(REQ):
            at_group = group
            at_slot = jnp.int32(r)
            for back in range(s, -1, -1):
                came = slot_ref[back, at_group] == at_slot
                source = wrap(at_group - shift_ref[back] + GROUPS)
                source_slot = slot_ref[back, source]
                at_group = jnp.where(came, source, at_group)
                at_slot = jnp.where(came, source_slot, at_slot)
            column = (at_group * REQ + at_slot) * 8 + s
            target = jnp.where((row & (ROWS - 1)) == s * REQ + r, column, target)
    target = target + jnp.where(row >= ROWS, 4, 0)
    for part in range(GROUPS * REQ * 8 // HD):
        pick_out_ref[:, part * HD : (part + 1) * HD] = jnp.where(
            target == lanes + part * HD, 1.0, 0.0
        ).astype(bf16)

    length = len_ref[own]
    angles = (length + (row8 & 3)).astype(f32) * freq_ref[...]
    sine = jnp.sin(angles)
    table_ref[:, 0:HD] = jnp.cos(angles)
    table_ref[:, HD : 2 * HD] = jnp.where(lane < HD // 2, -sine, sine)
    for part in range(CONTEXT // HD):
        table_ref[:, (2 + part) * HD : (3 + part) * HD] = jnp.where(
            lane + part * HD < length, 1.0, 0.0
        )
    for copy in large:
        copy.wait()


def project_kernel(
    x_ref,
    pick_ref,
    gain_ref,
    wkv_ref,
    kc_ref,
    vc_ref,
    wq0_ref,
    wq_hbm,
    out_ref,
    wq1_ref,
    wq2_ref,
    wq3_ref,
    sems,
):
    copies = []
    for k, part in enumerate((wq1_ref, wq2_ref, wq3_ref)):
        columns = pl.ds((1 + k) * part.shape[1], part.shape[1])
        copies.append(pltpu.make_async_copy(wq_hbm.at[:, columns], part, sems.at[k]))
        copies[k].start(priority=1)
    row8 = lax.broadcasted_iota(jnp.int32, (8, HD), 0)
    x = jnp.dot(pick_ref[...].astype(bf16), x_ref[...], preferred_element_type=f32)
    squares = jnp.sum(x * x, axis=-1, keepdims=True)
    normed = (x * gain_ref[...].astype(f32)).astype(bf16)
    squares = jnp.broadcast_to(squares, (8 * REQ, HD))
    high = squares.astype(bf16).astype(f32)
    lanes = lax.broadcasted_iota(jnp.int32, squares.shape, 1)
    squares = jnp.where(lanes < HD // 2, high, squares - high)
    for k, wq_ref in enumerate((wq0_ref, wq1_ref, wq2_ref, wq3_ref)):
        if k >= 1:
            copies[k - 1].wait()
        query = jnp.dot(normed, wq_ref[...], preferred_element_type=f32)
        key = jnp.dot(normed, wkv_ref[:, k * HD : (k + 1) * HD], preferred_element_type=f32)
        value = jnp.dot(
            normed,
            wkv_ref[:, KV_WIDTH + k * HD : KV_WIDTH + (k + 1) * HD],
            preferred_element_type=f32,
        )
        for r in range(REQ):
            rows = slice(r * 8, r * 8 + 8)
            tiles = [
                jnp.where(
                    row8 < 4,
                    query[rows, 2 * i * HD : (2 * i + 1) * HD],
                    query[rows, (2 * i + 1) * HD : (2 * i + 2) * HD],
                )
                for i in range(PER_KV // 2)
            ]
            tiles.append(jnp.where(row8 < 4, key[rows], value[rows]))
            tiles.append(squares[rows])
            at = k * REQ + r
            out_ref[at, 0:LOCAL, :] = kc_ref[r, :, k * HD : (k + 1) * HD]
            out_ref[at, LOCAL : 2 * LOCAL, :] = vc_ref[r, :, k * HD : (k + 1) * HD]
            out_ref[at, 2 * LOCAL : CHUNK, :] = jnp.concatenate(tiles, axis=0).astype(bf16)


def attend_kernel(table_ref, in_ref, out_ref):
    total = in_ref[0, 2 * LOCAL : CHUNK, :].astype(f32)
    for k in range(1, SEQ):
        total = total + in_ref[k, 2 * LOCAL : CHUNK, :].astype(f32)
    squares = jnp.sum(total[40:48], axis=-1, keepdims=True) * (2.0 / HD)
    inverse = lax.rsqrt(squares / D + norm_eps)
    cosine = table_ref[:, 0:HD]
    sine = table_ref[:, HD : 2 * HD]

    def rotated(tile):
        return tile * cosine + pltpu.roll(tile, HD // 2, 1) * sine

    query = jnp.concatenate(
        [rotated(total[i * 8 : i * 8 + 8] * inverse) for i in range(4)], axis=0
    ).astype(bf16)
    fresh = total[32:40] * inverse
    new_key = rotated(fresh)
    new_value = pltpu.roll(fresh, 4, 0)
    empty = jnp.zeros((HD - 8, HD), f32)
    new_key = jnp.concatenate([new_key, empty], axis=0).astype(bf16)
    new_value = jnp.concatenate([new_value, empty], axis=0).astype(bf16)

    keys = in_ref[:, 0:LOCAL, :].reshape(CONTEXT, HD)
    values = in_ref[:, LOCAL : 2 * LOCAL, :].reshape(CONTEXT, HD)
    scale = 1.0 / np.sqrt(np.float32(HD))
    contract = (((1,), (1,)), ((), ()))
    scores = lax.dot_general(query, keys, contract, preferred_element_type=f32) * scale
    recent = lax.dot_general(query, new_key, contract, preferred_element_type=f32) * scale
    live = jnp.broadcast_to(table_ref[0:1, 2 * HD : 2 * HD + CONTEXT], scores.shape)
    scores = jnp.where(live > 0.5, scores, masked_score)
    step = lax.broadcasted_iota(jnp.int32, recent.shape, 0) & 3
    recent = jnp.where(
        lax.broadcasted_iota(jnp.int32, recent.shape, 1) <= step, recent, masked_score
    )
    peak = jnp.maximum(
        jnp.max(scores, axis=-1, keepdims=True), jnp.max(recent, axis=-1, keepdims=True)
    )
    weights = jnp.exp(scores - peak)
    recent_weights = jnp.exp(recent - peak)
    count = jnp.sum(weights, axis=-1, keepdims=True) + jnp.sum(
        recent_weights, axis=-1, keepdims=True
    )
    summed = jnp.dot(weights.astype(bf16), values, preferred_element_type=f32) + jnp.dot(
        recent_weights.astype(bf16), new_value, preferred_element_type=f32
    )
    attention = (summed / count).astype(bf16)
    rows = attention.shape[0]
    for g in range(GROUPS):
        out_ref[g * rows : (g + 1) * rows, :] = attention


def output_kernel(pick_ref, in_ref, w_ref, out_ref):
    picked = jnp.dot(pick_ref[...], in_ref[...], preferred_element_type=f32)
    attention = jnp.concatenate([picked[0:ROWS], picked[ROWS : 2 * ROWS]], axis=1).astype(bf16)
    width = out_ref.shape[2]
    for k in range(SEQ):
        columns = slice(k * width, (k + 1) * width)
        out_ref[k] = jnp.dot(
            attention, w_ref[:, columns], preferred_element_type=f32
        ).astype(bf16)


def gather_kernel(in_ref, out_ref):
    total = in_ref[0].astype(f32)
    for k in range(1, SEQ):
        total = total + in_ref[k].astype(f32)
    for s in range(STEPS):
        out_ref[s] = total[s * REQ : (s + 1) * REQ].astype(bf16)


def body(
    step_inputs,
    norm_gain,
    w_query,
    w_keyval,
    w_out,
    key_cache,
    value_cache,
    ctx_len,
    mig_slot,
    mig_shift,
):
    width = step_inputs.shape[2]
    seq = ("seq_y", "seq_z")
    group = lax.axis_index("group").astype(jnp.int32).reshape(1)
    own = lax.axis_index("seq_z").astype(jnp.int32).reshape(1)

    x = pl.pallas_call(
        spread_kernel,
        in_specs=[anywhere()],
        out_specs=in_vmem(),
        out_shape=jax.ShapeDtypeStruct((GROUPS, ROWS, width), bf16),
        scratch_shapes=[pltpu.VMEM(step_inputs.shape, bf16), pltpu.SemaphoreType.DMA],
        compiler_params=params(),
        name="spread",
    )(left(step_inputs))
    x = lax.all_to_all(x, "group", 0, 0, tiled=True).reshape(GROUPS * ROWS, width)

    half = np.arange(HD) % (HD // 2)
    freq = jnp.asarray((rope_base ** (-2.0 * half / HD)).astype(np.float32).reshape(1, HD))
    large = (w_query, w_keyval, key_cache, value_cache)
    pick_in, pick_out, table, wkv, kc, vc, *split = pl.pallas_call(
        prepare_kernel,
        in_specs=[anywhere()] * 3
        + [pl.BlockSpec(memory_space=pltpu.SMEM)] * 2
        + [anywhere()] * 5,
        out_specs=[in_vmem()] * 7,
        out_shape=[
            pltpu.VMEM((8 * REQ, GROUPS * ROWS), f32),
            pltpu.VMEM((2 * ROWS, GROUPS * REQ * 8), bf16),
            pltpu.VMEM((8, 2 * HD + CONTEXT), f32),
        ]
        + [pltpu.VMEM(array.shape, bf16) for array in (w_keyval, key_cache, value_cache)]
        + [pltpu.VMEM((width, PER_KV * HD), bf16)],
        scratch_shapes=[
            pltpu.SMEM(mig_slot.shape, jnp.int32),
            pltpu.SMEM(mig_shift.shape, jnp.int32),
            pltpu.SMEM(ctx_len.shape, jnp.int32),
            pltpu.VMEM((1, HD), f32),
            pltpu.SemaphoreType.DMA((8,)),
        ],
        compiler_params=params(),
        cost_estimate=pl.CostEstimate(flops=0, bytes_accessed=20_000_000, transcendentals=0),
        name="prepare",
    )(
        left(mig_slot),
        left(mig_shift),
        left(ctx_len),
        group,
        own,
        left(freq),
        *[left(array) for array in large],
    )

    sent = pl.pallas_call(
        project_kernel,
        in_specs=[in_vmem()] * 7 + [anywhere()],
        out_specs=in_vmem(),
        out_shape=jax.ShapeDtypeStruct((SEQ, CHUNK, HD), bf16),
        scratch_shapes=[pltpu.VMEM((width, PER_KV * HD), bf16)] * 3
        + [pltpu.SemaphoreType.DMA((3,))],
        compiler_params=params(),
        name="project",
    )(
        x,
        placed(pick_in),
        norm_gain.reshape(1, width),
        placed(wkv),
        placed(kc),
        placed(vc),
        *[placed(part) for part in split],
        left(w_query),
    )
    received = lax.all_to_all(sent, seq, 0, 0, tiled=True)

    attention = pl.pallas_call(
        attend_kernel,
        in_specs=[in_vmem()] * 2,
        out_specs=in_vmem(),
        out_shape=jax.ShapeDtypeStruct((GROUPS * PER_KV * STEPS, HD), bf16),
        compiler_params=params(),
        name="attend",
    )(placed(table), received)
    attention = lax.all_to_all(
        attention.reshape(GROUPS * 4, 8, HD), ("group", "seq_z"), 0, 0, tiled=True
    ).reshape(GROUPS * 4 * 8, HD)

    shares = pl.pallas_call(
        output_kernel,
        in_specs=[in_vmem()] * 3,
        out_specs=in_vmem(),
        out_shape=jax.ShapeDtypeStruct((SEQ, ROWS, width), bf16),
        compiler_params=params(),
        name="output",
    )(placed(pick_out), attention, placed(w_out))
    shares = lax.all_to_all(shares, seq, 0, 0, tiled=True)
    return pl.pallas_call(
        gather_kernel,
        in_specs=[in_vmem()],
        out_specs=in_vmem(),
        out_shape=jax.ShapeDtypeStruct((STEPS, REQ, width), bf16),
        compiler_params=params(),
        name="gather",
    )(shares)


def solution(mesh):
    split = Mesh(mesh.devices.reshape(GROUPS, 4, 4), ("group", "seq_y", "seq_z"))
    seq = ("seq_y", "seq_z")
    specs = (
        P(None, "group", seq),
        P(seq),
        P(seq, None),
        P(seq, None),
        P(seq, None),
        P("group", seq, None),
        P("group", seq, None),
        P("group"),
        P(),
        P(),
    )
    return jax.shard_map(
        body, mesh=split, in_specs=specs, out_specs=P(None, "group", seq), check_vma=False
    )
```

```python
import jax
import jax.numpy as jnp
import numpy as np
from jax import lax
from jax.experimental import pallas as pl
from jax.experimental.pallas import tpu as pltpu
from jax.sharding import Mesh
from jax.sharding import PartitionSpec as P

D = 8192
H = 32
KVH = 4
HD = 128
STEPS = 4
REQ = 4
GROUPS = 16
SEQ = 16
PER_KV = H // KVH
LOCAL = 32
CONTEXT = SEQ * LOCAL
KV_WIDTH = KVH * HD
ROWS = STEPS * REQ
CHUNK = 2 * LOCAL + PER_KV * STEPS + 16

norm_eps = 1e-06
rope_base = 1000000.0
masked_score = -1e30

f32 = jnp.float32
bf16 = jnp.bfloat16


def anywhere():
    return pl.BlockSpec(memory_space=pl.ANY)


def in_vmem():
    return pl.BlockSpec(memory_space=pltpu.VMEM)


def params(mib=16):
    return pltpu.CompilerParams(vmem_limit_bytes=mib * 1024 * 1024)


def placed(array):
    return pltpu.with_memory_space_constraint(array, pltpu.VMEM)


def left(array):
    return pltpu.with_memory_space_constraint(array, pltpu.HBM)


def wrap(value):
    return jnp.where(value >= GROUPS, value - GROUPS, value)


def ring(value):
    return value ^ (value >> 1)


SEQ_ORDER = [ring(y) * 4 + ring(z) for y in range(4) for z in range(4)]


def spread_kernel(x_hbm, out_ref, x_ref, sem):
    copy = pltpu.make_async_copy(x_hbm, x_ref, sem)
    copy.start()
    copy.wait()
    x = jnp.concatenate([x_ref[s].astype(f32) for s in range(STEPS)], axis=0).astype(bf16)
    for g in range(GROUPS):
        out_ref[g] = x


def prepare_kernel(
    slot_hbm,
    shift_hbm,
    len_hbm,
    group_ref,
    own_ref,
    freq_hbm,
    wq_hbm,
    wkv_hbm,
    pick_in_ref,
    pick_out_ref,
    table_ref,
    wkv_ref,
    wq0_ref,
    wq1_ref,
    slot_ref,
    shift_ref,
    len_ref,
    freq_ref,
    sems,
):
    small = [
        pltpu.make_async_copy(slot_hbm, slot_ref, sems.at[0]),
        pltpu.make_async_copy(shift_hbm, shift_ref, sems.at[1]),
        pltpu.make_async_copy(len_hbm, len_ref, sems.at[2]),
        pltpu.make_async_copy(freq_hbm, freq_ref, sems.at[6]),
    ]
    large = [pltpu.make_async_copy(wkv_hbm, wkv_ref, sems.at[3])]
    for k, part in enumerate((wq0_ref, wq1_ref)):
        columns = pl.ds(k * part.shape[1], part.shape[1])
        large.append(pltpu.make_async_copy(wq_hbm.at[:, columns], part, sems.at[4 + k]))
    for copy in small + large:
        copy.start()
    for copy in small:
        copy.wait()
    group = group_ref[0]
    own = own_ref[0]

    row8 = lax.broadcasted_iota(jnp.int32, (8, HD), 0)
    lane = lax.broadcasted_iota(jnp.int32, (8, HD), 1)
    for r in range(REQ):
        at_group = group
        at_slot = jnp.int32(r)
        target = jnp.zeros((8, HD), jnp.int32)
        for s in range(STEPS):
            leaves = slot_ref[s, at_group] == at_slot
            next_group = wrap(at_group + shift_ref[s])
            next_slot = slot_ref[s, next_group]
            at_group = jnp.where(leaves, next_group, at_group)
            at_slot = jnp.where(leaves, next_slot, at_slot)
            column = at_group * ROWS + s * REQ + at_slot
            target = jnp.where((row8 & 3) == s, column, target)
        for part in range(GROUPS * ROWS // HD):
            pick_in_ref[r * 8 : r * 8 + 8, part * HD : (part + 1) * HD] = jnp.where(
                target == lane + part * HD, 1.0, 0.0
            )

    row = lax.broadcasted_iota(jnp.int32, (2 * ROWS, HD), 0)
    lanes = lax.broadcasted_iota(jnp.int32, (2 * ROWS, HD), 1)
    target = jnp.zeros((2 * ROWS, HD), jnp.int32)
    for s in range(STEPS):
        for r in range(REQ):
            at_group = group
            at_slot = jnp.int32(r)
            for back in range(s, -1, -1):
                came = slot_ref[back, at_group] == at_slot
                source = wrap(at_group - shift_ref[back] + GROUPS)
                source_slot = slot_ref[back, source]
                at_group = jnp.where(came, source, at_group)
                at_slot = jnp.where(came, source_slot, at_slot)
            column = (at_group * REQ + at_slot) * 8 + s
            target = jnp.where((row & (ROWS - 1)) == s * REQ + r, column, target)
    target = target + jnp.where(row >= ROWS, 4, 0)
    for part in range(GROUPS * REQ * 8 // HD):
        pick_out_ref[:, part * HD : (part + 1) * HD] = jnp.where(
            target == lanes + part * HD, 1.0, 0.0
        ).astype(bf16)

    length = len_ref[own]
    angles = (length + (row8 & 3)).astype(f32) * freq_ref[...]
    sine = jnp.sin(angles)
    table_ref[:, 0:HD] = jnp.cos(angles)
    table_ref[:, HD : 2 * HD] = jnp.where(lane < HD // 2, -sine, sine)
    for part in range(CONTEXT // HD):
        table_ref[:, (2 + part) * HD : (3 + part) * HD] = jnp.where(
            lane + part * HD < length, 1.0, 0.0
        )
    for copy in large:
        copy.wait()


def project_kernel(
    x_ref,
    pick_ref,
    gain_ref,
    wkv_ref,
    wq0_ref,
    wq1_ref,
    wq_hbm,
    kc_hbm,
    vc_hbm,
    out_ref,
    wq2_ref,
    wq3_ref,
    sems,
    cache_sems,
):
    copies = []
    for k, part in enumerate((wq2_ref, wq3_ref)):
        columns = pl.ds((2 + k) * part.shape[1], part.shape[1])
        copies.append(pltpu.make_async_copy(wq_hbm.at[:, columns], part, sems.at[k]))
        copies[k].start(priority=1)
    cached = []
    for k in range(KVH):
        for part, cache in enumerate((kc_hbm, vc_hbm)):
            source = cache.at[:, :, pl.ds(k * HD, HD)]
            target = out_ref.at[pl.ds(k * REQ, REQ), pl.ds(part * LOCAL, LOCAL), :]
            cached.append(pltpu.make_async_copy(source, target, cache_sems.at[2 * k + part]))
            cached[-1].start()
    row8 = lax.broadcasted_iota(jnp.int32, (8, HD), 0)
    x = jnp.dot(pick_ref[...].astype(bf16), x_ref[...], preferred_element_type=f32)
    squares = jnp.sum(x * x, axis=-1, keepdims=True)
    normed = (x * gain_ref[...].astype(f32)).astype(bf16)
    squares = jnp.broadcast_to(squares, (8 * REQ, HD))
    high = squares.astype(bf16).astype(f32)
    lanes = lax.broadcasted_iota(jnp.int32, squares.shape, 1)
    squares = jnp.where(lanes < HD // 2, high, squares - high)
    for k, wq_ref in enumerate((wq0_ref, wq1_ref, wq2_ref, wq3_ref)):
        if k >= 2:
            copies[k - 2].wait()
        query = jnp.dot(normed, wq_ref[...], preferred_element_type=f32)
        key = jnp.dot(normed, wkv_ref[:, k * HD : (k + 1) * HD], preferred_element_type=f32)
        value = jnp.dot(
            normed,
            wkv_ref[:, KV_WIDTH + k * HD : KV_WIDTH + (k + 1) * HD],
            preferred_element_type=f32,
        )
        for r in range(REQ):
            rows = slice(r * 8, r * 8 + 8)
            tiles = [
                jnp.where(
                    row8 < 4,
                    query[rows, 2 * i * HD : (2 * i + 1) * HD],
                    query[rows, (2 * i + 1) * HD : (2 * i + 2) * HD],
                )
                for i in range(PER_KV // 2)
            ]
            tiles.append(jnp.where(row8 < 4, key[rows], value[rows]))
            tiles.append(squares[rows])
            at = k * REQ + r
            out_ref[at, 2 * LOCAL : CHUNK, :] = jnp.concatenate(tiles, axis=0).astype(bf16)
    for copy in cached:
        copy.wait()


def attend_kernel(table_ref, in_ref, out_ref):
    total = in_ref[0, 2 * LOCAL : CHUNK, :].astype(f32)
    for k in range(1, SEQ):
        total = total + in_ref[k, 2 * LOCAL : CHUNK, :].astype(f32)
    squares = jnp.sum(total[40:48], axis=-1, keepdims=True) * (2.0 / HD)
    inverse = lax.rsqrt(squares / D + norm_eps)
    cosine = table_ref[:, 0:HD]
    sine = table_ref[:, HD : 2 * HD]

    def rotated(tile):
        return tile * cosine + pltpu.roll(tile, HD // 2, 1) * sine

    query = jnp.concatenate(
        [rotated(total[i * 8 : i * 8 + 8] * inverse) for i in range(4)], axis=0
    ).astype(bf16)
    fresh = total[32:40] * inverse
    new_key = rotated(fresh)
    new_value = pltpu.roll(fresh, 4, 0)
    empty = jnp.zeros((HD - 8, HD), f32)
    new_key = jnp.concatenate([new_key, empty], axis=0).astype(bf16)
    new_value = jnp.concatenate([new_value, empty], axis=0).astype(bf16)

    keys = in_ref[:, 0:LOCAL, :].reshape(CONTEXT, HD)
    values = in_ref[:, LOCAL : 2 * LOCAL, :].reshape(CONTEXT, HD)
    scale = 1.0 / np.sqrt(np.float32(HD))
    contract = (((1,), (1,)), ((), ()))
    scores = lax.dot_general(query, keys, contract, preferred_element_type=f32) * scale
    recent = lax.dot_general(query, new_key, contract, preferred_element_type=f32) * scale
    live = jnp.broadcast_to(table_ref[0:1, 2 * HD : 2 * HD + CONTEXT], scores.shape)
    scores = jnp.where(live > 0.5, scores, masked_score)
    step = lax.broadcasted_iota(jnp.int32, recent.shape, 0) & 3
    recent = jnp.where(
        lax.broadcasted_iota(jnp.int32, recent.shape, 1) <= step, recent, masked_score
    )
    peak = jnp.maximum(
        jnp.max(scores, axis=-1, keepdims=True), jnp.max(recent, axis=-1, keepdims=True)
    )
    weights = jnp.exp(scores - peak)
    recent_weights = jnp.exp(recent - peak)
    count = jnp.sum(weights, axis=-1, keepdims=True) + jnp.sum(
        recent_weights, axis=-1, keepdims=True
    )
    summed = jnp.dot(weights.astype(bf16), values, preferred_element_type=f32) + jnp.dot(
        recent_weights.astype(bf16), new_value, preferred_element_type=f32
    )
    attention = (summed / count).astype(bf16)
    rows = attention.shape[0]
    for g in range(GROUPS):
        out_ref[g * rows : (g + 1) * rows, :] = attention


def output_kernel(pick_ref, in_ref, w_ref, out_ref):
    picked = jnp.dot(pick_ref[...], in_ref[...], preferred_element_type=f32)
    attention = jnp.concatenate([picked[0:ROWS], picked[ROWS : 2 * ROWS]], axis=1).astype(bf16)
    width = out_ref.shape[2]
    for k in range(SEQ):
        columns = slice(k * width, (k + 1) * width)
        out_ref[SEQ_ORDER.index(k)] = jnp.dot(
            attention, w_ref[:, columns], preferred_element_type=f32
        ).astype(bf16)


def gather_kernel(in_ref, out_ref):
    total = in_ref[0].astype(f32)
    for k in range(1, SEQ):
        total = total + in_ref[k].astype(f32)
    for s in range(STEPS):
        out_ref[s] = total[s * REQ : (s + 1) * REQ].astype(bf16)


def body(
    step_inputs,
    norm_gain,
    w_query,
    w_keyval,
    w_out,
    key_cache,
    value_cache,
    ctx_len,
    mig_slot,
    mig_shift,
):
    width = step_inputs.shape[2]
    seq = ("seq_y", "seq_z")
    group = lax.axis_index("group").astype(jnp.int32).reshape(1)
    own = lax.axis_index("seq_z").astype(jnp.int32).reshape(1)

    x = pl.pallas_call(
        spread_kernel,
        in_specs=[anywhere()],
        out_specs=in_vmem(),
        out_shape=jax.ShapeDtypeStruct((GROUPS, ROWS, width), bf16),
        scratch_shapes=[pltpu.VMEM(step_inputs.shape, bf16), pltpu.SemaphoreType.DMA],
        compiler_params=params(),
        name="spread",
    )(left(step_inputs))
    x = lax.all_to_all(x, "group", 0, 0, tiled=True).reshape(GROUPS * ROWS, width)

    half = np.arange(HD) % (HD // 2)
    freq = jnp.asarray((rope_base ** (-2.0 * half / HD)).astype(np.float32).reshape(1, HD))
    large = (w_query, w_keyval)
    pick_in, pick_out, table, wkv, *split = pl.pallas_call(
        prepare_kernel,
        in_specs=[anywhere()] * 3
        + [pl.BlockSpec(memory_space=pltpu.SMEM)] * 2
        + [anywhere()] * 3,
        out_specs=[in_vmem()] * 6,
        out_shape=[
            pltpu.VMEM((8 * REQ, GROUPS * ROWS), f32),
            pltpu.VMEM((2 * ROWS, GROUPS * REQ * 8), bf16),
            pltpu.VMEM((8, 2 * HD + CONTEXT), f32),
        ]
        + [pltpu.VMEM(w_keyval.shape, bf16)]
        + [pltpu.VMEM((width, PER_KV * HD), bf16)] * 2,
        scratch_shapes=[
            pltpu.SMEM(mig_slot.shape, jnp.int32),
            pltpu.SMEM(mig_shift.shape, jnp.int32),
            pltpu.SMEM(ctx_len.shape, jnp.int32),
            pltpu.VMEM((1, HD), f32),
            pltpu.SemaphoreType.DMA((7,)),
        ],
        compiler_params=params(),
        cost_estimate=pl.CostEstimate(flops=0, bytes_accessed=20_000_000, transcendentals=0),
        name="prepare",
    )(
        left(mig_slot),
        left(mig_shift),
        left(ctx_len),
        group,
        own,
        left(freq),
        *[left(array) for array in large],
    )

    sent = pl.pallas_call(
        project_kernel,
        in_specs=[in_vmem()] * 6 + [anywhere()] * 3,
        out_specs=in_vmem(),
        out_shape=jax.ShapeDtypeStruct((SEQ, CHUNK, HD), bf16),
        scratch_shapes=[pltpu.VMEM((width, PER_KV * HD), bf16)] * 2
        + [pltpu.SemaphoreType.DMA((2,)), pltpu.SemaphoreType.DMA((2 * KVH,))],
        compiler_params=params(),
        name="project",
    )(
        x,
        placed(pick_in),
        norm_gain.reshape(1, width),
        placed(wkv),
        *[placed(part) for part in split],
        left(w_query),
        left(key_cache),
        left(value_cache),
    )
    received = lax.all_to_all(sent, seq, 0, 0, tiled=True)

    attention = pl.pallas_call(
        attend_kernel,
        in_specs=[in_vmem()] * 2,
        out_specs=in_vmem(),
        out_shape=jax.ShapeDtypeStruct((GROUPS * PER_KV * STEPS, HD), bf16),
        compiler_params=params(),
        name="attend",
    )(placed(table), received)
    attention = lax.all_to_all(
        attention.reshape(GROUPS * 4, 8, HD), ("group", "seq_z"), 0, 0, tiled=True
    ).reshape(GROUPS * 4 * 8, HD)

    shares = pl.pallas_call(
        output_kernel,
        in_specs=[in_vmem()] * 3,
        out_specs=in_vmem(),
        out_shape=jax.ShapeDtypeStruct((SEQ, ROWS, width), bf16),
        compiler_params=params(),
        name="output",
    )(placed(pick_out), attention, placed(w_out))
    shares = lax.all_to_all(
        shares, seq, 0, 0, tiled=True, axis_index_groups=[SEQ_ORDER]
    )
    return pl.pallas_call(
        gather_kernel,
        in_specs=[in_vmem()],
        out_specs=in_vmem(),
        out_shape=jax.ShapeDtypeStruct((STEPS, REQ, width), bf16),
        compiler_params=params(),
        name="gather",
    )(shares)


def solution(mesh):
    split = Mesh(mesh.devices.reshape(GROUPS, 4, 4), ("group", "seq_y", "seq_z"))
    seq = ("seq_y", "seq_z")
    specs = (
        P(None, "group", seq),
        P(seq),
        P(seq, None),
        P(seq, None),
        P(seq, None),
        P("group", seq, None),
        P("group", seq, None),
        P("group"),
        P(),
        P(),
    )
    return jax.shard_map(
        body, mesh=split, in_specs=specs, out_specs=P(None, "group", seq), check_vma=False
    )
```

```python
import jax
import jax.numpy as jnp
import numpy as np
from jax import lax
from jax.experimental import pallas as pl
from jax.experimental.pallas import tpu as pltpu
from jax.sharding import Mesh
from jax.sharding import PartitionSpec as P

D = 8192
H = 32
KVH = 4
HD = 128
STEPS = 4
REQ = 4
GROUPS = 16
SEQ = 16
PER_KV = H // KVH
LOCAL = 32
CONTEXT = SEQ * LOCAL
KV_WIDTH = KVH * HD
ROWS = STEPS * REQ
CHUNK = 2 * LOCAL + PER_KV * STEPS + 16

norm_eps = 1e-06
rope_base = 1000000.0
masked_score = -1e30

f32 = jnp.float32
bf16 = jnp.bfloat16


def anywhere():
    return pl.BlockSpec(memory_space=pl.ANY)


def in_vmem():
    return pl.BlockSpec(memory_space=pltpu.VMEM)


def params(mib=16):
    return pltpu.CompilerParams(vmem_limit_bytes=mib * 1024 * 1024)


def placed(array):
    return pltpu.with_memory_space_constraint(array, pltpu.VMEM)


def left(array):
    return pltpu.with_memory_space_constraint(array, pltpu.HBM)


def wrap(value):
    return jnp.where(value >= GROUPS, value - GROUPS, value)


SEQ_ORDER = [4 * y + (z if y % 2 == 0 else 3 - z) for y in range(4) for z in range(4)]


def spread_kernel(x_hbm, out_ref, x_ref, sem):
    copy = pltpu.make_async_copy(x_hbm, x_ref, sem)
    copy.start()
    copy.wait()
    x = jnp.concatenate([x_ref[s].astype(f32) for s in range(STEPS)], axis=0).astype(bf16)
    for g in range(GROUPS):
        out_ref[g] = x


def prepare_kernel(
    slot_hbm,
    shift_hbm,
    len_hbm,
    group_ref,
    own_ref,
    freq_hbm,
    wq_hbm,
    wkv_hbm,
    pick_in_ref,
    pick_out_ref,
    table_ref,
    wkv_ref,
    wq0_ref,
    wq1_ref,
    slot_ref,
    shift_ref,
    len_ref,
    freq_ref,
    sems,
):
    small = [
        pltpu.make_async_copy(slot_hbm, slot_ref, sems.at[0]),
        pltpu.make_async_copy(shift_hbm, shift_ref, sems.at[1]),
        pltpu.make_async_copy(len_hbm, len_ref, sems.at[2]),
        pltpu.make_async_copy(freq_hbm, freq_ref, sems.at[6]),
    ]
    large = [pltpu.make_async_copy(wkv_hbm, wkv_ref, sems.at[3])]
    for k, part in enumerate((wq0_ref, wq1_ref)):
        columns = pl.ds(k * part.shape[1], part.shape[1])
        large.append(pltpu.make_async_copy(wq_hbm.at[:, columns], part, sems.at[4 + k]))
    for copy in small + large:
        copy.start()
    for copy in small:
        copy.wait()
    group = group_ref[0]
    own = own_ref[0]

    row8 = lax.broadcasted_iota(jnp.int32, (8, HD), 0)
    lane = lax.broadcasted_iota(jnp.int32, (8, HD), 1)
    for r in range(REQ):
        at_group = group
        at_slot = jnp.int32(r)
        target = jnp.zeros((8, HD), jnp.int32)
        for s in range(STEPS):
            leaves = slot_ref[s, at_group] == at_slot
            next_group = wrap(at_group + shift_ref[s])
            next_slot = slot_ref[s, next_group]
            at_group = jnp.where(leaves, next_group, at_group)
            at_slot = jnp.where(leaves, next_slot, at_slot)
            column = at_group * ROWS + s * REQ + at_slot
            target = jnp.where((row8 & 3) == s, column, target)
        for part in range(GROUPS * ROWS // HD):
            pick_in_ref[r * 8 : r * 8 + 8, part * HD : (part + 1) * HD] = jnp.where(
                target == lane + part * HD, 1.0, 0.0
            )

    row = lax.broadcasted_iota(jnp.int32, (2 * ROWS, HD), 0)
    lanes = lax.broadcasted_iota(jnp.int32, (2 * ROWS, HD), 1)
    target = jnp.zeros((2 * ROWS, HD), jnp.int32)
    for s in range(STEPS):
        for r in range(REQ):
            at_group = group
            at_slot = jnp.int32(r)
            for back in range(s, -1, -1):
                came = slot_ref[back, at_group] == at_slot
                source = wrap(at_group - shift_ref[back] + GROUPS)
                source_slot = slot_ref[back, source]
                at_group = jnp.where(came, source, at_group)
                at_slot = jnp.where(came, source_slot, at_slot)
            column = (at_group * REQ + at_slot) * 8 + s
            target = jnp.where((row & (ROWS - 1)) == s * REQ + r, column, target)
    target = target + jnp.where(row >= ROWS, 4, 0)
    for part in range(GROUPS * REQ * 8 // HD):
        pick_out_ref[:, part * HD : (part + 1) * HD] = jnp.where(
            target == lanes + part * HD, 1.0, 0.0
        ).astype(bf16)

    length = len_ref[own]
    angles = (length + (row8 & 3)).astype(f32) * freq_ref[...]
    sine = jnp.sin(angles)
    table_ref[:, 0:HD] = jnp.cos(angles)
    table_ref[:, HD : 2 * HD] = jnp.where(lane < HD // 2, -sine, sine)
    for part in range(CONTEXT // HD):
        table_ref[:, (2 + part) * HD : (3 + part) * HD] = jnp.where(
            lane + part * HD < length, 1.0, 0.0
        )
    for copy in large:
        copy.wait()


def project_kernel(
    x_ref,
    pick_ref,
    gain_ref,
    wkv_ref,
    wq0_ref,
    wq1_ref,
    wq_hbm,
    kc_hbm,
    vc_hbm,
    out_ref,
    wq2_ref,
    wq3_ref,
    sems,
    cache_sems,
):
    copies = []
    for k, part in enumerate((wq2_ref, wq3_ref)):
        columns = pl.ds((2 + k) * part.shape[1], part.shape[1])
        copies.append(pltpu.make_async_copy(wq_hbm.at[:, columns], part, sems.at[k]))
        copies[k].start(priority=1)
    cached = []
    for k in range(KVH):
        for part, cache in enumerate((kc_hbm, vc_hbm)):
            source = cache.at[:, :, pl.ds(k * HD, HD)]
            target = out_ref.at[pl.ds(k * REQ, REQ), pl.ds(part * LOCAL, LOCAL), :]
            cached.append(pltpu.make_async_copy(source, target, cache_sems.at[2 * k + part]))
            cached[-1].start()
    row8 = lax.broadcasted_iota(jnp.int32, (8, HD), 0)
    x = jnp.dot(pick_ref[...].astype(bf16), x_ref[...], preferred_element_type=f32)
    squares = jnp.sum(x * x, axis=-1, keepdims=True)
    normed = (x * gain_ref[...].astype(f32)).astype(bf16)
    squares = jnp.broadcast_to(squares, (8 * REQ, HD))
    high = squares.astype(bf16).astype(f32)
    lanes = lax.broadcasted_iota(jnp.int32, squares.shape, 1)
    squares = jnp.where(lanes < HD // 2, high, squares - high)
    for k, wq_ref in enumerate((wq0_ref, wq1_ref, wq2_ref, wq3_ref)):
        if k >= 2:
            copies[k - 2].wait()
        query = jnp.dot(normed, wq_ref[...], preferred_element_type=f32)
        key = jnp.dot(normed, wkv_ref[:, k * HD : (k + 1) * HD], preferred_element_type=f32)
        value = jnp.dot(
            normed,
            wkv_ref[:, KV_WIDTH + k * HD : KV_WIDTH + (k + 1) * HD],
            preferred_element_type=f32,
        )
        for r in range(REQ):
            rows = slice(r * 8, r * 8 + 8)
            tiles = [
                jnp.where(
                    row8 < 4,
                    query[rows, 2 * i * HD : (2 * i + 1) * HD],
                    query[rows, (2 * i + 1) * HD : (2 * i + 2) * HD],
                )
                for i in range(PER_KV // 2)
            ]
            tiles.append(jnp.where(row8 < 4, key[rows], value[rows]))
            tiles.append(squares[rows])
            at = k * REQ + r
            out_ref[at, 2 * LOCAL : CHUNK, :] = jnp.concatenate(tiles, axis=0).astype(bf16)
    for copy in cached:
        copy.wait()


def attend_kernel(table_ref, in_ref, out_ref):
    total = in_ref[0, 2 * LOCAL : CHUNK, :].astype(f32)
    for k in range(1, SEQ):
        total = total + in_ref[k, 2 * LOCAL : CHUNK, :].astype(f32)
    squares = jnp.sum(total[40:48], axis=-1, keepdims=True) * (2.0 / HD)
    inverse = lax.rsqrt(squares / D + norm_eps)
    cosine = table_ref[:, 0:HD]
    sine = table_ref[:, HD : 2 * HD]

    def rotated(tile):
        return tile * cosine + pltpu.roll(tile, HD // 2, 1) * sine

    query = jnp.concatenate(
        [rotated(total[i * 8 : i * 8 + 8] * inverse) for i in range(4)], axis=0
    ).astype(bf16)
    fresh = total[32:40] * inverse
    new_key = rotated(fresh)
    new_value = pltpu.roll(fresh, 4, 0)
    empty = jnp.zeros((HD - 8, HD), f32)
    new_key = jnp.concatenate([new_key, empty], axis=0).astype(bf16)
    new_value = jnp.concatenate([new_value, empty], axis=0).astype(bf16)

    keys = in_ref[:, 0:LOCAL, :].reshape(CONTEXT, HD)
    values = in_ref[:, LOCAL : 2 * LOCAL, :].reshape(CONTEXT, HD)
    scale = 1.0 / np.sqrt(np.float32(HD))
    contract = (((1,), (1,)), ((), ()))
    scores = lax.dot_general(query, keys, contract, preferred_element_type=f32) * scale
    recent = lax.dot_general(query, new_key, contract, preferred_element_type=f32) * scale
    live = jnp.broadcast_to(table_ref[0:1, 2 * HD : 2 * HD + CONTEXT], scores.shape)
    scores = jnp.where(live > 0.5, scores, masked_score)
    step = lax.broadcasted_iota(jnp.int32, recent.shape, 0) & 3
    recent = jnp.where(
        lax.broadcasted_iota(jnp.int32, recent.shape, 1) <= step, recent, masked_score
    )
    peak = jnp.maximum(
        jnp.max(scores, axis=-1, keepdims=True), jnp.max(recent, axis=-1, keepdims=True)
    )
    weights = jnp.exp(scores - peak)
    recent_weights = jnp.exp(recent - peak)
    count = jnp.sum(weights, axis=-1, keepdims=True) + jnp.sum(
        recent_weights, axis=-1, keepdims=True
    )
    summed = jnp.dot(weights.astype(bf16), values, preferred_element_type=f32) + jnp.dot(
        recent_weights.astype(bf16), new_value, preferred_element_type=f32
    )
    attention = (summed / count).astype(bf16)
    rows = attention.shape[0]
    for g in range(GROUPS):
        out_ref[g * rows : (g + 1) * rows, :] = attention


def output_kernel(pick_ref, in_ref, w_ref, out_ref):
    picked = jnp.dot(pick_ref[...], in_ref[...], preferred_element_type=f32)
    attention = jnp.concatenate([picked[0:ROWS], picked[ROWS : 2 * ROWS]], axis=1).astype(bf16)
    width = out_ref.shape[2]
    for k in range(SEQ):
        columns = slice(k * width, (k + 1) * width)
        out_ref[SEQ_ORDER.index(k)] = jnp.dot(
            attention, w_ref[:, columns], preferred_element_type=f32
        ).astype(bf16)


def gather_kernel(in_ref, out_ref):
    total = in_ref[0].astype(f32)
    for k in range(1, SEQ):
        total = total + in_ref[k].astype(f32)
    for s in range(STEPS):
        out_ref[s] = total[s * REQ : (s + 1) * REQ].astype(bf16)


def body(
    step_inputs,
    norm_gain,
    w_query,
    w_keyval,
    w_out,
    key_cache,
    value_cache,
    ctx_len,
    mig_slot,
    mig_shift,
):
    width = step_inputs.shape[2]
    seq = ("seq_y", "seq_z")
    group = lax.axis_index("group").astype(jnp.int32).reshape(1)
    own = lax.axis_index("seq_z").astype(jnp.int32).reshape(1)

    x = pl.pallas_call(
        spread_kernel,
        in_specs=[anywhere()],
        out_specs=in_vmem(),
        out_shape=jax.ShapeDtypeStruct((GROUPS, ROWS, width), bf16),
        scratch_shapes=[pltpu.VMEM(step_inputs.shape, bf16), pltpu.SemaphoreType.DMA],
        compiler_params=params(),
        name="spread",
    )(left(step_inputs))
    x = lax.all_to_all(x, "group", 0, 0, tiled=True).reshape(GROUPS * ROWS, width)

    half = np.arange(HD) % (HD // 2)
    freq = jnp.asarray((rope_base ** (-2.0 * half / HD)).astype(np.float32).reshape(1, HD))
    large = (w_query, w_keyval)
    pick_in, pick_out, table, wkv, *split = pl.pallas_call(
        prepare_kernel,
        in_specs=[anywhere()] * 3
        + [pl.BlockSpec(memory_space=pltpu.SMEM)] * 2
        + [anywhere()] * 3,
        out_specs=[in_vmem()] * 6,
        out_shape=[
            pltpu.VMEM((8 * REQ, GROUPS * ROWS), f32),
            pltpu.VMEM((2 * ROWS, GROUPS * REQ * 8), bf16),
            pltpu.VMEM((8, 2 * HD + CONTEXT), f32),
        ]
        + [pltpu.VMEM(w_keyval.shape, bf16)]
        + [pltpu.VMEM((width, PER_KV * HD), bf16)] * 2,
        scratch_shapes=[
            pltpu.SMEM(mig_slot.shape, jnp.int32),
            pltpu.SMEM(mig_shift.shape, jnp.int32),
            pltpu.SMEM(ctx_len.shape, jnp.int32),
            pltpu.VMEM((1, HD), f32),
            pltpu.SemaphoreType.DMA((7,)),
        ],
        compiler_params=params(),
        cost_estimate=pl.CostEstimate(flops=0, bytes_accessed=20_000_000, transcendentals=0),
        name="prepare",
    )(
        left(mig_slot),
        left(mig_shift),
        left(ctx_len),
        group,
        own,
        left(freq),
        *[left(array) for array in large],
    )

    sent = pl.pallas_call(
        project_kernel,
        in_specs=[in_vmem()] * 6 + [anywhere()] * 3,
        out_specs=in_vmem(),
        out_shape=jax.ShapeDtypeStruct((SEQ, CHUNK, HD), bf16),
        scratch_shapes=[pltpu.VMEM((width, PER_KV * HD), bf16)] * 2
        + [pltpu.SemaphoreType.DMA((2,)), pltpu.SemaphoreType.DMA((2 * KVH,))],
        compiler_params=params(),
        name="project",
    )(
        x,
        placed(pick_in),
        norm_gain.reshape(1, width),
        placed(wkv),
        *[placed(part) for part in split],
        left(w_query),
        left(key_cache),
        left(value_cache),
    )
    received = lax.all_to_all(sent, seq, 0, 0, tiled=True)

    attention = pl.pallas_call(
        attend_kernel,
        in_specs=[in_vmem()] * 2,
        out_specs=in_vmem(),
        out_shape=jax.ShapeDtypeStruct((GROUPS * PER_KV * STEPS, HD), bf16),
        compiler_params=params(),
        name="attend",
    )(placed(table), received)
    attention = lax.all_to_all(
        attention.reshape(GROUPS * 4, 8, HD), ("group", "seq_z"), 0, 0, tiled=True
    ).reshape(GROUPS * 4 * 8, HD)

    shares = pl.pallas_call(
        output_kernel,
        in_specs=[in_vmem()] * 3,
        out_specs=in_vmem(),
        out_shape=jax.ShapeDtypeStruct((SEQ, ROWS, width), bf16),
        compiler_params=params(),
        name="output",
    )(placed(pick_out), attention, placed(w_out))
    shares = lax.all_to_all(
        shares, seq, 0, 0, tiled=True, axis_index_groups=[SEQ_ORDER]
    )
    return pl.pallas_call(
        gather_kernel,
        in_specs=[in_vmem()],
        out_specs=in_vmem(),
        out_shape=jax.ShapeDtypeStruct((STEPS, REQ, width), bf16),
        compiler_params=params(),
        name="gather",
    )(shares)


def solution(mesh):
    split = Mesh(mesh.devices.reshape(GROUPS, 4, 4), ("group", "seq_y", "seq_z"))
    seq = ("seq_y", "seq_z")
    specs = (
        P(None, "group", seq),
        P(seq),
        P(seq, None),
        P(seq, None),
        P(seq, None),
        P("group", seq, None),
        P("group", seq, None),
        P("group"),
        P(),
        P(),
    )
    return jax.shard_map(
        body, mesh=split, in_specs=specs, out_specs=P(None, "group", seq), check_vma=False
    )
```

```python
import jax
import jax.numpy as jnp
import numpy as np
from jax import lax
from jax.experimental import pallas as pl
from jax.experimental.pallas import tpu as pltpu
from jax.sharding import Mesh
from jax.sharding import PartitionSpec as P

D = 8192
H = 32
KVH = 4
HD = 128
STEPS = 4
REQ = 4
GROUPS = 16
SEQ = 16
CHIPS = GROUPS // 2
PER_KV = H // KVH
LOCAL = 32
CONTEXT = SEQ * LOCAL
KV_WIDTH = KVH * HD
ROWS = STEPS * REQ
CHUNK = 2 * LOCAL + PER_KV * STEPS + 16

norm_eps = 1e-06
rope_base = 1000000.0
masked_score = -1e30

f32 = jnp.float32
bf16 = jnp.bfloat16


def anywhere():
    return pl.BlockSpec(memory_space=pl.ANY)


def in_vmem():
    return pl.BlockSpec(memory_space=pltpu.VMEM)


def params(mib=16):
    return pltpu.CompilerParams(vmem_limit_bytes=mib * 1024 * 1024)


def placed(array):
    return pltpu.with_memory_space_constraint(array, pltpu.VMEM)


def left(array):
    return pltpu.with_memory_space_constraint(array, pltpu.HBM)


def wrap(value):
    return jnp.where(value >= GROUPS, value - GROUPS, value)


SEQ_ORDER = [4 * y + (z if y % 2 == 0 else 3 - z) for y in range(4) for z in range(4)]


def spread_kernel(x_hbm, out_ref, x_ref, sem):
    copy = pltpu.make_async_copy(x_hbm, x_ref, sem)
    copy.start()
    copy.wait()
    x = jnp.concatenate([x_ref[s].astype(f32) for s in range(STEPS)], axis=0).astype(bf16)
    for g in range(GROUPS):
        out_ref[g] = x


def prepare_kernel(
    slot_hbm,
    shift_hbm,
    len_hbm,
    group_ref,
    own_ref,
    freq_hbm,
    wq_hbm,
    wkv_hbm,
    pick_in_ref,
    pick_out_ref,
    table_ref,
    wkv_ref,
    wq0_ref,
    wq1_ref,
    slot_ref,
    shift_ref,
    len_ref,
    freq_ref,
    sems,
):
    small = [
        pltpu.make_async_copy(slot_hbm, slot_ref, sems.at[0]),
        pltpu.make_async_copy(shift_hbm, shift_ref, sems.at[1]),
        pltpu.make_async_copy(len_hbm, len_ref, sems.at[2]),
        pltpu.make_async_copy(freq_hbm, freq_ref, sems.at[6]),
    ]
    large = [pltpu.make_async_copy(wkv_hbm, wkv_ref, sems.at[3])]
    for k, part in enumerate((wq0_ref, wq1_ref)):
        columns = pl.ds(k * part.shape[1], part.shape[1])
        large.append(pltpu.make_async_copy(wq_hbm.at[:, columns], part, sems.at[4 + k]))
    for copy in small + large:
        copy.start()
    for copy in small:
        copy.wait()
    group = group_ref[0]
    own = own_ref[0]

    row8 = lax.broadcasted_iota(jnp.int32, (8, HD), 0)
    lane = lax.broadcasted_iota(jnp.int32, (8, HD), 1)
    for r in range(REQ):
        at_group = group
        at_slot = jnp.int32(r)
        target = jnp.zeros((8, HD), jnp.int32)
        for s in range(STEPS):
            leaves = slot_ref[s, at_group] == at_slot
            next_group = wrap(at_group + shift_ref[s])
            next_slot = slot_ref[s, next_group]
            at_group = jnp.where(leaves, next_group, at_group)
            at_slot = jnp.where(leaves, next_slot, at_slot)
            column = at_group * ROWS + s * REQ + at_slot
            target = jnp.where((row8 & 3) == s, column, target)
        for part in range(GROUPS * ROWS // HD):
            pick_in_ref[r * 8 : r * 8 + 8, part * HD : (part + 1) * HD] = jnp.where(
                target == lane + part * HD, 1.0, 0.0
            )

    row = lax.broadcasted_iota(jnp.int32, (2 * ROWS, HD), 0)
    lanes = lax.broadcasted_iota(jnp.int32, (2 * ROWS, HD), 1)
    target = jnp.zeros((2 * ROWS, HD), jnp.int32)
    for s in range(STEPS):
        for r in range(REQ):
            at_group = group
            at_slot = jnp.int32(r)
            for back in range(s, -1, -1):
                came = slot_ref[back, at_group] == at_slot
                source = wrap(at_group - shift_ref[back] + GROUPS)
                source_slot = slot_ref[back, source]
                at_group = jnp.where(came, source, at_group)
                at_slot = jnp.where(came, source_slot, at_slot)
            column = ((at_group >> 1) * REQ + at_slot) * 8 + s
            column = column + ((at_group ^ group) & 1) * (CHIPS * REQ * 8)
            target = jnp.where((row & (ROWS - 1)) == s * REQ + r, column, target)
    target = target + jnp.where(row >= ROWS, 4, 0)
    for part in range(GROUPS * REQ * 8 // HD):
        pick_out_ref[:, part * HD : (part + 1) * HD] = jnp.where(
            target == lanes + part * HD, 1.0, 0.0
        ).astype(bf16)

    length = len_ref[own]
    angles = (length + (row8 & 3)).astype(f32) * freq_ref[...]
    sine = jnp.sin(angles)
    table_ref[:, 0:HD] = jnp.cos(angles)
    table_ref[:, HD : 2 * HD] = jnp.where(lane < HD // 2, -sine, sine)
    for part in range(CONTEXT // HD):
        table_ref[:, (2 + part) * HD : (3 + part) * HD] = jnp.where(
            lane + part * HD < length, 1.0, 0.0
        )
    for copy in large:
        copy.wait()


def project_kernel(
    x_ref,
    pick_ref,
    gain_ref,
    wkv_ref,
    wq0_ref,
    wq1_ref,
    wq_hbm,
    kc_hbm,
    vc_hbm,
    out_ref,
    wq2_ref,
    wq3_ref,
    sems,
    cache_sems,
):
    copies = []
    for k, part in enumerate((wq2_ref, wq3_ref)):
        columns = pl.ds((2 + k) * part.shape[1], part.shape[1])
        copies.append(pltpu.make_async_copy(wq_hbm.at[:, columns], part, sems.at[k]))
        copies[k].start(priority=1)
    cached = []
    for k in range(KVH):
        for part, cache in enumerate((kc_hbm, vc_hbm)):
            source = cache.at[:, :, pl.ds(k * HD, HD)]
            target = out_ref.at[pl.ds(k * REQ, REQ), pl.ds(part * LOCAL, LOCAL), :]
            cached.append(pltpu.make_async_copy(source, target, cache_sems.at[2 * k + part]))
            cached[-1].start()
    row8 = lax.broadcasted_iota(jnp.int32, (8, HD), 0)
    x = jnp.dot(pick_ref[...].astype(bf16), x_ref[...], preferred_element_type=f32)
    squares = jnp.sum(x * x, axis=-1, keepdims=True)
    normed = (x * gain_ref[...].astype(f32)).astype(bf16)
    squares = jnp.broadcast_to(squares, (8 * REQ, HD))
    high = squares.astype(bf16).astype(f32)
    lanes = lax.broadcasted_iota(jnp.int32, squares.shape, 1)
    squares = jnp.where(lanes < HD // 2, high, squares - high)
    for k, wq_ref in enumerate((wq0_ref, wq1_ref, wq2_ref, wq3_ref)):
        if k >= 2:
            copies[k - 2].wait()
        query = jnp.dot(normed, wq_ref[...], preferred_element_type=f32)
        key = jnp.dot(normed, wkv_ref[:, k * HD : (k + 1) * HD], preferred_element_type=f32)
        value = jnp.dot(
            normed,
            wkv_ref[:, KV_WIDTH + k * HD : KV_WIDTH + (k + 1) * HD],
            preferred_element_type=f32,
        )
        for r in range(REQ):
            rows = slice(r * 8, r * 8 + 8)
            tiles = [
                jnp.where(
                    row8 < 4,
                    query[rows, 2 * i * HD : (2 * i + 1) * HD],
                    query[rows, (2 * i + 1) * HD : (2 * i + 2) * HD],
                )
                for i in range(PER_KV // 2)
            ]
            tiles.append(jnp.where(row8 < 4, key[rows], value[rows]))
            tiles.append(squares[rows])
            at = k * REQ + r
            out_ref[at, 2 * LOCAL : CHUNK, :] = jnp.concatenate(tiles, axis=0).astype(bf16)
    for copy in cached:
        copy.wait()


def attend_kernel(table_ref, in_ref, out_ref):
    total = in_ref[0, 2 * LOCAL : CHUNK, :].astype(f32)
    for k in range(1, SEQ):
        total = total + in_ref[k, 2 * LOCAL : CHUNK, :].astype(f32)
    squares = jnp.sum(total[40:48], axis=-1, keepdims=True) * (2.0 / HD)
    inverse = lax.rsqrt(squares / D + norm_eps)
    cosine = table_ref[:, 0:HD]
    sine = table_ref[:, HD : 2 * HD]

    def rotated(tile):
        return tile * cosine + pltpu.roll(tile, HD // 2, 1) * sine

    query = jnp.concatenate(
        [rotated(total[i * 8 : i * 8 + 8] * inverse) for i in range(4)], axis=0
    ).astype(bf16)
    fresh = total[32:40] * inverse
    new_key = rotated(fresh)
    new_value = pltpu.roll(fresh, 4, 0)
    empty = jnp.zeros((HD - 8, HD), f32)
    new_key = jnp.concatenate([new_key, empty], axis=0).astype(bf16)
    new_value = jnp.concatenate([new_value, empty], axis=0).astype(bf16)

    keys = in_ref[:, 0:LOCAL, :].reshape(CONTEXT, HD)
    values = in_ref[:, LOCAL : 2 * LOCAL, :].reshape(CONTEXT, HD)
    scale = 1.0 / np.sqrt(np.float32(HD))
    contract = (((1,), (1,)), ((), ()))
    scores = lax.dot_general(query, keys, contract, preferred_element_type=f32) * scale
    recent = lax.dot_general(query, new_key, contract, preferred_element_type=f32) * scale
    live = jnp.broadcast_to(table_ref[0:1, 2 * HD : 2 * HD + CONTEXT], scores.shape)
    scores = jnp.where(live > 0.5, scores, masked_score)
    step = lax.broadcasted_iota(jnp.int32, recent.shape, 0) & 3
    recent = jnp.where(
        lax.broadcasted_iota(jnp.int32, recent.shape, 1) <= step, recent, masked_score
    )
    peak = jnp.maximum(
        jnp.max(scores, axis=-1, keepdims=True), jnp.max(recent, axis=-1, keepdims=True)
    )
    weights = jnp.exp(scores - peak)
    recent_weights = jnp.exp(recent - peak)
    count = jnp.sum(weights, axis=-1, keepdims=True) + jnp.sum(
        recent_weights, axis=-1, keepdims=True
    )
    summed = jnp.dot(weights.astype(bf16), values, preferred_element_type=f32) + jnp.dot(
        recent_weights.astype(bf16), new_value, preferred_element_type=f32
    )
    attention = (summed / count).astype(bf16)
    rows = attention.shape[0]
    for g in range(CHIPS):
        out_ref[g * rows : (g + 1) * rows, :] = attention


def output_kernel(pick_ref, in_ref, other_ref, w_ref, out_ref):
    half = CHIPS * REQ * 8
    picked = jnp.dot(pick_ref[:, :half], in_ref[...], preferred_element_type=f32)
    picked = picked + jnp.dot(pick_ref[:, half:], other_ref[...], preferred_element_type=f32)
    attention = jnp.concatenate([picked[0:ROWS], picked[ROWS : 2 * ROWS]], axis=1).astype(bf16)
    width = out_ref.shape[2]
    for k in range(SEQ):
        columns = slice(k * width, (k + 1) * width)
        out_ref[SEQ_ORDER.index(k)] = jnp.dot(
            attention, w_ref[:, columns], preferred_element_type=f32
        ).astype(bf16)


def gather_kernel(in_ref, out_ref):
    total = in_ref[0].astype(f32)
    for k in range(1, SEQ):
        total = total + in_ref[k].astype(f32)
    for s in range(STEPS):
        out_ref[s] = total[s * REQ : (s + 1) * REQ].astype(bf16)


def body(
    step_inputs,
    norm_gain,
    w_query,
    w_keyval,
    w_out,
    key_cache,
    value_cache,
    ctx_len,
    mig_slot,
    mig_shift,
):
    width = step_inputs.shape[2]
    seq = ("seq_y", "seq_z")
    group = lax.axis_index(("chip", "core")).astype(jnp.int32).reshape(1)
    own = lax.axis_index("seq_z").astype(jnp.int32).reshape(1)

    x = pl.pallas_call(
        spread_kernel,
        in_specs=[anywhere()],
        out_specs=in_vmem(),
        out_shape=jax.ShapeDtypeStruct((GROUPS, ROWS, width), bf16),
        scratch_shapes=[pltpu.VMEM(step_inputs.shape, bf16), pltpu.SemaphoreType.DMA],
        compiler_params=params(),
        name="spread",
    )(left(step_inputs))
    x = lax.all_to_all(x, ("chip", "core"), 0, 0, tiled=True).reshape(GROUPS * ROWS, width)

    half = np.arange(HD) % (HD // 2)
    freq = jnp.asarray((rope_base ** (-2.0 * half / HD)).astype(np.float32).reshape(1, HD))
    large = (w_query, w_keyval)
    pick_in, pick_out, table, wkv, *split = pl.pallas_call(
        prepare_kernel,
        in_specs=[anywhere()] * 3
        + [pl.BlockSpec(memory_space=pltpu.SMEM)] * 2
        + [anywhere()] * 3,
        out_specs=[in_vmem()] * 6,
        out_shape=[
            pltpu.VMEM((8 * REQ, GROUPS * ROWS), f32),
            pltpu.VMEM((2 * ROWS, GROUPS * REQ * 8), bf16),
            pltpu.VMEM((8, 2 * HD + CONTEXT), f32),
        ]
        + [pltpu.VMEM(w_keyval.shape, bf16)]
        + [pltpu.VMEM((width, PER_KV * HD), bf16)] * 2,
        scratch_shapes=[
            pltpu.SMEM(mig_slot.shape, jnp.int32),
            pltpu.SMEM(mig_shift.shape, jnp.int32),
            pltpu.SMEM(ctx_len.shape, jnp.int32),
            pltpu.VMEM((1, HD), f32),
            pltpu.SemaphoreType.DMA((7,)),
        ],
        compiler_params=params(),
        cost_estimate=pl.CostEstimate(flops=0, bytes_accessed=20_000_000, transcendentals=0),
        name="prepare",
    )(
        left(mig_slot),
        left(mig_shift),
        left(ctx_len),
        group,
        own,
        left(freq),
        *[left(array) for array in large],
    )

    sent = pl.pallas_call(
        project_kernel,
        in_specs=[in_vmem()] * 6 + [anywhere()] * 3,
        out_specs=in_vmem(),
        out_shape=jax.ShapeDtypeStruct((SEQ, CHUNK, HD), bf16),
        scratch_shapes=[pltpu.VMEM((width, PER_KV * HD), bf16)] * 2
        + [pltpu.SemaphoreType.DMA((2,)), pltpu.SemaphoreType.DMA((2 * KVH,))],
        compiler_params=params(),
        name="project",
    )(
        x,
        placed(pick_in),
        norm_gain.reshape(1, width),
        placed(wkv),
        *[placed(part) for part in split],
        left(w_query),
        left(key_cache),
        left(value_cache),
    )
    received = lax.all_to_all(sent, seq, 0, 0, tiled=True)

    attention = pl.pallas_call(
        attend_kernel,
        in_specs=[in_vmem()] * 2,
        out_specs=in_vmem(),
        out_shape=jax.ShapeDtypeStruct((CHIPS * PER_KV * STEPS, HD), bf16),
        compiler_params=params(),
        name="attend",
    )(placed(table), received)
    attention = lax.all_to_all(
        attention.reshape(CHIPS * 4, 8, HD), ("chip", "seq_z"), 0, 0, tiled=True
    ).reshape(CHIPS * 4 * 8, HD)
    other = lax.ppermute(attention, "core", [(0, 1), (1, 0)])

    shares = pl.pallas_call(
        output_kernel,
        in_specs=[in_vmem()] * 4,
        out_specs=in_vmem(),
        out_shape=jax.ShapeDtypeStruct((SEQ, ROWS, width), bf16),
        compiler_params=params(),
        name="output",
    )(placed(pick_out), attention, other, placed(w_out))
    shares = lax.all_to_all(
        shares, seq, 0, 0, tiled=True, axis_index_groups=[SEQ_ORDER]
    )
    return pl.pallas_call(
        gather_kernel,
        in_specs=[in_vmem()],
        out_specs=in_vmem(),
        out_shape=jax.ShapeDtypeStruct((STEPS, REQ, width), bf16),
        compiler_params=params(),
        name="gather",
    )(shares)


def solution(mesh):
    split = Mesh(mesh.devices.reshape(GROUPS // 2, 2, 4, 4), ("chip", "core", "seq_y", "seq_z"))
    seq = ("seq_y", "seq_z")
    group = ("chip", "core")
    specs = (
        P(None, group, seq),
        P(seq),
        P(seq, None),
        P(seq, None),
        P(seq, None),
        P(group, seq, None),
        P(group, seq, None),
        P(group),
        P(),
        P(),
    )
    return jax.shard_map(
        body, mesh=split, in_specs=specs, out_specs=P(None, group, seq), check_vma=False
    )
```

```python
import jax
import jax.numpy as jnp
import numpy as np
from jax import lax
from jax.experimental import pallas as pl
from jax.experimental.pallas import tpu as pltpu
from jax.sharding import Mesh
from jax.sharding import PartitionSpec as P

D = 8192
H = 32
KVH = 4
HD = 128
STEPS = 4
REQ = 4
GROUPS = 16
SEQ = 16
CHIPS = GROUPS // 2
PER_KV = H // KVH
LOCAL = 32
CONTEXT = SEQ * LOCAL
KV_WIDTH = KVH * HD
ROWS = STEPS * REQ
CHUNK = 2 * LOCAL + PER_KV * STEPS + 16

norm_eps = 1e-06
rope_base = 1000000.0
masked_score = -1e30

f32 = jnp.float32
bf16 = jnp.bfloat16


def anywhere():
    return pl.BlockSpec(memory_space=pl.ANY)


def in_vmem():
    return pl.BlockSpec(memory_space=pltpu.VMEM)


def params(mib=16):
    return pltpu.CompilerParams(vmem_limit_bytes=mib * 1024 * 1024)


def placed(array):
    return pltpu.with_memory_space_constraint(array, pltpu.VMEM)


def left(array):
    return pltpu.with_memory_space_constraint(array, pltpu.HBM)


def wrap(value):
    return jnp.where(value >= GROUPS, value - GROUPS, value)


SEQ_ORDER = [4 * y + (z if y % 2 == 0 else 3 - z) for y in range(4) for z in range(4)]


def spread_kernel(x_hbm, out_ref, x_ref, sem):
    copy = pltpu.make_async_copy(x_hbm, x_ref, sem)
    copy.start()
    copy.wait()
    x = jnp.concatenate([x_ref[s].astype(f32) for s in range(STEPS)], axis=0).astype(bf16)
    for g in range(GROUPS):
        out_ref[g] = x


def prepare_kernel(
    slot_hbm,
    shift_hbm,
    len_hbm,
    group_ref,
    own_ref,
    freq_hbm,
    wq_hbm,
    wkv_hbm,
    pick_in_ref,
    pick_out_ref,
    table_ref,
    wkv_ref,
    wq0_ref,
    wq1_ref,
    slot_ref,
    shift_ref,
    len_ref,
    freq_ref,
    sems,
):
    small = [
        pltpu.make_async_copy(slot_hbm, slot_ref, sems.at[0]),
        pltpu.make_async_copy(shift_hbm, shift_ref, sems.at[1]),
        pltpu.make_async_copy(len_hbm, len_ref, sems.at[2]),
        pltpu.make_async_copy(freq_hbm, freq_ref, sems.at[6]),
    ]
    large = [pltpu.make_async_copy(wkv_hbm, wkv_ref, sems.at[3])]
    for k, part in enumerate((wq0_ref, wq1_ref)):
        columns = pl.ds(k * part.shape[1], part.shape[1])
        large.append(pltpu.make_async_copy(wq_hbm.at[:, columns], part, sems.at[4 + k]))
    for copy in small + large:
        copy.start()
    for copy in small:
        copy.wait()
    group = group_ref[0]
    own = own_ref[0]

    row8 = lax.broadcasted_iota(jnp.int32, (8, HD), 0)
    lane = lax.broadcasted_iota(jnp.int32, (8, HD), 1)
    for r in range(REQ):
        at_group = group
        at_slot = jnp.int32(r)
        target = jnp.zeros((8, HD), jnp.int32)
        for s in range(STEPS):
            leaves = slot_ref[s, at_group] == at_slot
            next_group = wrap(at_group + shift_ref[s])
            next_slot = slot_ref[s, next_group]
            at_group = jnp.where(leaves, next_group, at_group)
            at_slot = jnp.where(leaves, next_slot, at_slot)
            column = at_group * ROWS + s * REQ + at_slot
            target = jnp.where((row8 & 3) == s, column, target)
        for part in range(GROUPS * ROWS // HD):
            pick_in_ref[r * 8 : r * 8 + 8, part * HD : (part + 1) * HD] = jnp.where(
                target == lane + part * HD, 1.0, 0.0
            )

    row = lax.broadcasted_iota(jnp.int32, (2 * ROWS, HD), 0)
    lanes = lax.broadcasted_iota(jnp.int32, (2 * ROWS, HD), 1)
    target = jnp.zeros((2 * ROWS, HD), jnp.int32)
    for s in range(STEPS):
        for r in range(REQ):
            at_group = group
            at_slot = jnp.int32(r)
            for back in range(s, -1, -1):
                came = slot_ref[back, at_group] == at_slot
                source = wrap(at_group - shift_ref[back] + GROUPS)
                source_slot = slot_ref[back, source]
                at_group = jnp.where(came, source, at_group)
                at_slot = jnp.where(came, source_slot, at_slot)
            column = ((at_group >> 1) * REQ + at_slot) * 8 + s
            column = column + ((at_group ^ group) & 1) * (CHIPS * REQ * 8)
            target = jnp.where((row & (ROWS - 1)) == s * REQ + r, column, target)
    target = target + jnp.where(row >= ROWS, 4, 0)
    for part in range(GROUPS * REQ * 8 // HD):
        pick_out_ref[:, part * HD : (part + 1) * HD] = jnp.where(
            target == lanes + part * HD, 1.0, 0.0
        ).astype(bf16)

    length = len_ref[own]
    angles = (length + (row8 & 3)).astype(f32) * freq_ref[...]
    sine = jnp.sin(angles)
    table_ref[:, 0:HD] = jnp.cos(angles)
    table_ref[:, HD : 2 * HD] = jnp.where(lane < HD // 2, -sine, sine)
    for part in range(CONTEXT // HD):
        table_ref[:, (2 + part) * HD : (3 + part) * HD] = jnp.where(
            lane + part * HD < length, 1.0, 0.0
        )
    for copy in large:
        copy.wait()


def project_kernel(
    x_ref,
    pick_ref,
    gain_ref,
    wkv_ref,
    wq0_ref,
    wq1_ref,
    wq_hbm,
    kc_hbm,
    vc_hbm,
    out_ref,
    wq2_ref,
    wq3_ref,
    sems,
    cache_sems,
):
    copies = []
    for k, part in enumerate((wq2_ref, wq3_ref)):
        columns = pl.ds((2 + k) * part.shape[1], part.shape[1])
        copies.append(pltpu.make_async_copy(wq_hbm.at[:, columns], part, sems.at[k]))
        copies[k].start()
    cached = []
    for k in range(KVH):
        for part, cache in enumerate((kc_hbm, vc_hbm)):
            source = cache.at[:, :, pl.ds(k * HD, HD)]
            target = out_ref.at[pl.ds(k * REQ, REQ), pl.ds(part * LOCAL, LOCAL), :]
            cached.append(pltpu.make_async_copy(source, target, cache_sems.at[2 * k + part]))
            cached[-1].start()
    row8 = lax.broadcasted_iota(jnp.int32, (8, HD), 0)
    x = jnp.dot(pick_ref[...].astype(bf16), x_ref[...], preferred_element_type=f32)
    squares = jnp.sum(x * x, axis=-1, keepdims=True)
    normed = (x * gain_ref[...].astype(f32)).astype(bf16)
    squares = jnp.broadcast_to(squares, (8 * REQ, HD))
    high = squares.astype(bf16).astype(f32)
    lanes = lax.broadcasted_iota(jnp.int32, squares.shape, 1)
    squares = jnp.where(lanes < HD // 2, high, squares - high)
    for k, wq_ref in enumerate((wq0_ref, wq1_ref, wq2_ref, wq3_ref)):
        if k >= 2:
            copies[k - 2].wait()
        query = jnp.dot(normed, wq_ref[...], preferred_element_type=f32)
        key = jnp.dot(normed, wkv_ref[:, k * HD : (k + 1) * HD], preferred_element_type=f32)
        value = jnp.dot(
            normed,
            wkv_ref[:, KV_WIDTH + k * HD : KV_WIDTH + (k + 1) * HD],
            preferred_element_type=f32,
        )
        for r in range(REQ):
            rows = slice(r * 8, r * 8 + 8)
            tiles = [
                jnp.where(
                    row8 < 4,
                    query[rows, 2 * i * HD : (2 * i + 1) * HD],
                    query[rows, (2 * i + 1) * HD : (2 * i + 2) * HD],
                )
                for i in range(PER_KV // 2)
            ]
            tiles.append(jnp.where(row8 < 4, key[rows], value[rows]))
            tiles.append(squares[rows])
            at = k * REQ + r
            out_ref[at, 2 * LOCAL : CHUNK, :] = jnp.concatenate(tiles, axis=0).astype(bf16)
    for copy in cached:
        copy.wait()


def attend_kernel(table_ref, in_ref, out_ref):
    total = in_ref[0, 2 * LOCAL : CHUNK, :].astype(f32)
    for k in range(1, SEQ):
        total = total + in_ref[k, 2 * LOCAL : CHUNK, :].astype(f32)
    squares = jnp.sum(total[40:48], axis=-1, keepdims=True) * (2.0 / HD)
    inverse = lax.rsqrt(squares / D + norm_eps)
    cosine = table_ref[:, 0:HD]
    sine = table_ref[:, HD : 2 * HD]

    def rotated(tile):
        return tile * cosine + pltpu.roll(tile, HD // 2, 1) * sine

    query = jnp.concatenate(
        [rotated(total[i * 8 : i * 8 + 8] * inverse) for i in range(4)], axis=0
    ).astype(bf16)
    fresh = total[32:40] * inverse
    new_key = rotated(fresh)
    new_value = pltpu.roll(fresh, 4, 0)
    empty = jnp.zeros((HD - 8, HD), f32)
    new_key = jnp.concatenate([new_key, empty], axis=0).astype(bf16)
    new_value = jnp.concatenate([new_value, empty], axis=0).astype(bf16)

    keys = in_ref[:, 0:LOCAL, :].reshape(CONTEXT, HD)
    values = in_ref[:, LOCAL : 2 * LOCAL, :].reshape(CONTEXT, HD)
    scale = 1.0 / np.sqrt(np.float32(HD))
    contract = (((1,), (1,)), ((), ()))
    scores = lax.dot_general(query, keys, contract, preferred_element_type=f32) * scale
    recent = lax.dot_general(query, new_key, contract, preferred_element_type=f32) * scale
    live = jnp.broadcast_to(table_ref[0:1, 2 * HD : 2 * HD + CONTEXT], scores.shape)
    scores = jnp.where(live > 0.5, scores, masked_score)
    step = lax.broadcasted_iota(jnp.int32, recent.shape, 0) & 3
    recent = jnp.where(
        lax.broadcasted_iota(jnp.int32, recent.shape, 1) <= step, recent, masked_score
    )
    peak = jnp.maximum(
        jnp.max(scores, axis=-1, keepdims=True), jnp.max(recent, axis=-1, keepdims=True)
    )
    weights = jnp.exp(scores - peak)
    recent_weights = jnp.exp(recent - peak)
    count = jnp.sum(weights, axis=-1, keepdims=True) + jnp.sum(
        recent_weights, axis=-1, keepdims=True
    )
    summed = jnp.dot(weights.astype(bf16), values, preferred_element_type=f32) + jnp.dot(
        recent_weights.astype(bf16), new_value, preferred_element_type=f32
    )
    attention = (summed / count).astype(bf16)
    rows = attention.shape[0]
    for g in range(CHIPS):
        out_ref[g * rows : (g + 1) * rows, :] = attention


def output_kernel(pick_ref, in_ref, other_ref, w_ref, out_ref):
    half = CHIPS * REQ * 8
    picked = jnp.dot(pick_ref[:, :half], in_ref[...], preferred_element_type=f32)
    picked = picked + jnp.dot(pick_ref[:, half:], other_ref[...], preferred_element_type=f32)
    attention = jnp.concatenate([picked[0:ROWS], picked[ROWS : 2 * ROWS]], axis=1).astype(bf16)
    width = out_ref.shape[2]
    for k in range(SEQ):
        columns = slice(k * width, (k + 1) * width)
        out_ref[SEQ_ORDER.index(k)] = jnp.dot(
            attention, w_ref[:, columns], preferred_element_type=f32
        ).astype(bf16)


def gather_kernel(in_ref, out_ref):
    total = in_ref[0].astype(f32)
    for k in range(1, SEQ):
        total = total + in_ref[k].astype(f32)
    for s in range(STEPS):
        out_ref[s] = total[s * REQ : (s + 1) * REQ].astype(bf16)


def body(
    step_inputs,
    norm_gain,
    w_query,
    w_keyval,
    w_out,
    key_cache,
    value_cache,
    ctx_len,
    mig_slot,
    mig_shift,
):
    width = step_inputs.shape[2]
    seq = ("seq_y", "seq_z")
    group = lax.axis_index(("chip", "core")).astype(jnp.int32).reshape(1)
    own = lax.axis_index("seq_z").astype(jnp.int32).reshape(1)

    x = pl.pallas_call(
        spread_kernel,
        in_specs=[anywhere()],
        out_specs=in_vmem(),
        out_shape=jax.ShapeDtypeStruct((GROUPS, ROWS, width), bf16),
        scratch_shapes=[pltpu.VMEM(step_inputs.shape, bf16), pltpu.SemaphoreType.DMA],
        compiler_params=params(),
        name="spread",
    )(left(step_inputs))
    x = lax.all_to_all(x, ("chip", "core"), 0, 0, tiled=True).reshape(GROUPS * ROWS, width)

    half = np.arange(HD) % (HD // 2)
    freq = jnp.asarray((rope_base ** (-2.0 * half / HD)).astype(np.float32).reshape(1, HD))
    large = (w_query, w_keyval)
    pick_in, pick_out, table, wkv, *split = pl.pallas_call(
        prepare_kernel,
        in_specs=[anywhere()] * 3
        + [pl.BlockSpec(memory_space=pltpu.SMEM)] * 2
        + [anywhere()] * 3,
        out_specs=[in_vmem()] * 6,
        out_shape=[
            pltpu.VMEM((8 * REQ, GROUPS * ROWS), f32),
            pltpu.VMEM((2 * ROWS, GROUPS * REQ * 8), bf16),
            pltpu.VMEM((8, 2 * HD + CONTEXT), f32),
        ]
        + [pltpu.VMEM(w_keyval.shape, bf16)]
        + [pltpu.VMEM((width, PER_KV * HD), bf16)] * 2,
        scratch_shapes=[
            pltpu.SMEM(mig_slot.shape, jnp.int32),
            pltpu.SMEM(mig_shift.shape, jnp.int32),
            pltpu.SMEM(ctx_len.shape, jnp.int32),
            pltpu.VMEM((1, HD), f32),
            pltpu.SemaphoreType.DMA((7,)),
        ],
        compiler_params=params(),
        cost_estimate=pl.CostEstimate(flops=0, bytes_accessed=20_000_000, transcendentals=0),
        name="prepare",
    )(
        left(mig_slot),
        left(mig_shift),
        left(ctx_len),
        group,
        own,
        left(freq),
        *[left(array) for array in large],
    )

    sent = pl.pallas_call(
        project_kernel,
        in_specs=[in_vmem()] * 6 + [anywhere()] * 3,
        out_specs=in_vmem(),
        out_shape=jax.ShapeDtypeStruct((SEQ, CHUNK, HD), bf16),
        scratch_shapes=[pltpu.VMEM((width, PER_KV * HD), bf16)] * 2
        + [pltpu.SemaphoreType.DMA((2,)), pltpu.SemaphoreType.DMA((2 * KVH,))],
        compiler_params=params(),
        name="project",
    )(
        x,
        placed(pick_in),
        norm_gain.reshape(1, width),
        placed(wkv),
        *[placed(part) for part in split],
        left(w_query),
        left(key_cache),
        left(value_cache),
    )
    received = lax.all_to_all(sent, seq, 0, 0, tiled=True)

    attention = pl.pallas_call(
        attend_kernel,
        in_specs=[in_vmem()] * 2,
        out_specs=in_vmem(),
        out_shape=jax.ShapeDtypeStruct((CHIPS * PER_KV * STEPS, HD), bf16),
        compiler_params=params(),
        name="attend",
    )(placed(table), received)
    attention = lax.all_to_all(
        attention.reshape(CHIPS * 4, 8, HD), ("chip", "seq_z"), 0, 0, tiled=True
    ).reshape(CHIPS * 4 * 8, HD)
    other = lax.ppermute(attention, "core", [(0, 1), (1, 0)])

    shares = pl.pallas_call(
        output_kernel,
        in_specs=[in_vmem()] * 4,
        out_specs=in_vmem(),
        out_shape=jax.ShapeDtypeStruct((SEQ, ROWS, width), bf16),
        compiler_params=params(),
        name="output",
    )(placed(pick_out), attention, other, placed(w_out))
    shares = lax.all_to_all(
        shares, seq, 0, 0, tiled=True, axis_index_groups=[SEQ_ORDER]
    )
    return pl.pallas_call(
        gather_kernel,
        in_specs=[in_vmem()],
        out_specs=in_vmem(),
        out_shape=jax.ShapeDtypeStruct((STEPS, REQ, width), bf16),
        compiler_params=params(),
        name="gather",
    )(shares)


def solution(mesh):
    split = Mesh(mesh.devices.reshape(GROUPS // 2, 2, 4, 4), ("chip", "core", "seq_y", "seq_z"))
    seq = ("seq_y", "seq_z")
    group = ("chip", "core")
    specs = (
        P(None, group, seq),
        P(seq),
        P(seq, None),
        P(seq, None),
        P(seq, None),
        P(group, seq, None),
        P(group, seq, None),
        P(group),
        P(),
        P(),
    )
    return jax.shard_map(
        body, mesh=split, in_specs=specs, out_specs=P(None, group, seq), check_vma=False
    )
```

```python
import jax
import jax.numpy as jnp
import numpy as np
from jax import lax
from jax.experimental import pallas as pl
from jax.experimental.pallas import tpu as pltpu
from jax.sharding import Mesh
from jax.sharding import PartitionSpec as P

D = 8192
H = 32
KVH = 4
HD = 128
STEPS = 4
REQ = 4
GROUPS = 16
SEQ = 16
CHIPS = GROUPS // 2
PER_KV = H // KVH
LOCAL = 32
CONTEXT = SEQ * LOCAL
KV_WIDTH = KVH * HD
ROWS = STEPS * REQ
CHUNK = 2 * LOCAL + PER_KV * STEPS + 16

norm_eps = 1e-06
rope_base = 1000000.0
masked_score = -1e30

f32 = jnp.float32
bf16 = jnp.bfloat16


def anywhere():
    return pl.BlockSpec(memory_space=pl.ANY)


def in_vmem():
    return pl.BlockSpec(memory_space=pltpu.VMEM)


def params(mib=16):
    return pltpu.CompilerParams(vmem_limit_bytes=mib * 1024 * 1024)


def placed(array):
    return pltpu.with_memory_space_constraint(array, pltpu.VMEM)


def left(array):
    return pltpu.with_memory_space_constraint(array, pltpu.HBM)


def wrap(value):
    return jnp.where(value >= GROUPS, value - GROUPS, value)


SEQ_ORDER = [4 * y + (z if y % 2 == 0 else 3 - z) for y in range(4) for z in range(4)]


def spread_kernel(x_hbm, out_ref, x_ref, sem):
    copy = pltpu.make_async_copy(x_hbm, x_ref, sem)
    copy.start()
    copy.wait()
    x = jnp.concatenate([x_ref[s].astype(f32) for s in range(STEPS)], axis=0).astype(bf16)
    for g in range(GROUPS):
        out_ref[g] = x


def prepare_kernel(
    slot_hbm,
    shift_hbm,
    len_hbm,
    group_ref,
    own_ref,
    freq_hbm,
    wq_hbm,
    wkv_hbm,
    pick_in_ref,
    pick_out_ref,
    table_ref,
    wkv_ref,
    wq0_ref,
    wq1_ref,
    slot_ref,
    shift_ref,
    len_ref,
    freq_ref,
    sems,
):
    small = [
        pltpu.make_async_copy(slot_hbm, slot_ref, sems.at[0]),
        pltpu.make_async_copy(shift_hbm, shift_ref, sems.at[1]),
        pltpu.make_async_copy(len_hbm, len_ref, sems.at[2]),
        pltpu.make_async_copy(freq_hbm, freq_ref, sems.at[6]),
    ]
    large = [pltpu.make_async_copy(wkv_hbm, wkv_ref, sems.at[3])]
    for k, part in enumerate((wq0_ref, wq1_ref)):
        columns = pl.ds(k * part.shape[1], part.shape[1])
        large.append(pltpu.make_async_copy(wq_hbm.at[:, columns], part, sems.at[4 + k]))
    for copy in small + large:
        copy.start()
    for copy in small:
        copy.wait()
    group = group_ref[0]
    own = own_ref[0]

    row8 = lax.broadcasted_iota(jnp.int32, (8, HD), 0)
    lane = lax.broadcasted_iota(jnp.int32, (8, HD), 1)
    for r in range(REQ):
        at_group = group
        at_slot = jnp.int32(r)
        target = jnp.zeros((8, HD), jnp.int32)
        for s in range(STEPS):
            leaves = slot_ref[s, at_group] == at_slot
            next_group = wrap(at_group + shift_ref[s])
            next_slot = slot_ref[s, next_group]
            at_group = jnp.where(leaves, next_group, at_group)
            at_slot = jnp.where(leaves, next_slot, at_slot)
            along = at_group >> 2
            place = (along ^ (along >> 1)) * 4 + (at_group & 3)
            column = place * ROWS + s * REQ + at_slot
            target = jnp.where((row8 & 3) == s, column, target)
        for part in range(GROUPS * ROWS // HD):
            pick_in_ref[r * 8 : r * 8 + 8, part * HD : (part + 1) * HD] = jnp.where(
                target == lane + part * HD, 1.0, 0.0
            )

    row = lax.broadcasted_iota(jnp.int32, (2 * ROWS, HD), 0)
    lanes = lax.broadcasted_iota(jnp.int32, (2 * ROWS, HD), 1)
    target = jnp.zeros((2 * ROWS, HD), jnp.int32)
    for s in range(STEPS):
        for r in range(REQ):
            at_group = group
            at_slot = jnp.int32(r)
            for back in range(s, -1, -1):
                came = slot_ref[back, at_group] == at_slot
                source = wrap(at_group - shift_ref[back] + GROUPS)
                source_slot = slot_ref[back, source]
                at_group = jnp.where(came, source, at_group)
                at_slot = jnp.where(came, source_slot, at_slot)
            column = ((at_group >> 1) * REQ + at_slot) * 8 + s
            column = column + ((at_group ^ group) & 1) * (CHIPS * REQ * 8)
            target = jnp.where((row & (ROWS - 1)) == s * REQ + r, column, target)
    target = target + jnp.where(row >= ROWS, 4, 0)
    for part in range(GROUPS * REQ * 8 // HD):
        pick_out_ref[:, part * HD : (part + 1) * HD] = jnp.where(
            target == lanes + part * HD, 1.0, 0.0
        ).astype(bf16)

    length = len_ref[own]
    angles = (length + (row8 & 3)).astype(f32) * freq_ref[...]
    sine = jnp.sin(angles)
    table_ref[:, 0:HD] = jnp.cos(angles)
    table_ref[:, HD : 2 * HD] = jnp.where(lane < HD // 2, -sine, sine)
    for part in range(CONTEXT // HD):
        table_ref[:, (2 + part) * HD : (3 + part) * HD] = jnp.where(
            lane + part * HD < length, 1.0, 0.0
        )
    for copy in large:
        copy.wait()


def project_kernel(
    x_ref,
    pick_ref,
    gain_ref,
    wkv_ref,
    wq0_ref,
    wq1_ref,
    wq_hbm,
    kc_hbm,
    vc_hbm,
    out_ref,
    wq2_ref,
    wq3_ref,
    sems,
    cache_sems,
):
    copies = []
    for k, part in enumerate((wq2_ref, wq3_ref)):
        columns = pl.ds((2 + k) * part.shape[1], part.shape[1])
        copies.append(pltpu.make_async_copy(wq_hbm.at[:, columns], part, sems.at[k]))
        copies[k].start()
    cached = []
    for k in range(KVH):
        for part, cache in enumerate((kc_hbm, vc_hbm)):
            source = cache.at[:, :, pl.ds(k * HD, HD)]
            target = out_ref.at[pl.ds(k * REQ, REQ), pl.ds(part * LOCAL, LOCAL), :]
            cached.append(pltpu.make_async_copy(source, target, cache_sems.at[2 * k + part]))
            cached[-1].start()
    row8 = lax.broadcasted_iota(jnp.int32, (8, HD), 0)
    x = jnp.dot(pick_ref[...].astype(bf16), x_ref[...], preferred_element_type=f32)
    squares = jnp.sum(x * x, axis=-1, keepdims=True)
    normed = (x * gain_ref[...].astype(f32)).astype(bf16)
    squares = jnp.broadcast_to(squares, (8 * REQ, HD))
    high = squares.astype(bf16).astype(f32)
    lanes = lax.broadcasted_iota(jnp.int32, squares.shape, 1)
    squares = jnp.where(lanes < HD // 2, high, squares - high)
    for k, wq_ref in enumerate((wq0_ref, wq1_ref, wq2_ref, wq3_ref)):
        if k >= 2:
            copies[k - 2].wait()
        query = jnp.dot(normed, wq_ref[...], preferred_element_type=f32)
        key = jnp.dot(normed, wkv_ref[:, k * HD : (k + 1) * HD], preferred_element_type=f32)
        value = jnp.dot(
            normed,
            wkv_ref[:, KV_WIDTH + k * HD : KV_WIDTH + (k + 1) * HD],
            preferred_element_type=f32,
        )
        for r in range(REQ):
            rows = slice(r * 8, r * 8 + 8)
            tiles = [
                jnp.where(
                    row8 < 4,
                    query[rows, 2 * i * HD : (2 * i + 1) * HD],
                    query[rows, (2 * i + 1) * HD : (2 * i + 2) * HD],
                )
                for i in range(PER_KV // 2)
            ]
            tiles.append(jnp.where(row8 < 4, key[rows], value[rows]))
            tiles.append(squares[rows])
            at = k * REQ + r
            out_ref[at, 2 * LOCAL : CHUNK, :] = jnp.concatenate(tiles, axis=0).astype(bf16)
    for copy in cached:
        copy.wait()


def attend_kernel(table_ref, in_ref, out_ref):
    total = in_ref[0, 2 * LOCAL : CHUNK, :].astype(f32)
    for k in range(1, SEQ):
        total = total + in_ref[k, 2 * LOCAL : CHUNK, :].astype(f32)
    squares = jnp.sum(total[40:48], axis=-1, keepdims=True) * (2.0 / HD)
    inverse = lax.rsqrt(squares / D + norm_eps)
    cosine = table_ref[:, 0:HD]
    sine = table_ref[:, HD : 2 * HD]

    def rotated(tile):
        return tile * cosine + pltpu.roll(tile, HD // 2, 1) * sine

    query = jnp.concatenate(
        [rotated(total[i * 8 : i * 8 + 8] * inverse) for i in range(4)], axis=0
    ).astype(bf16)
    fresh = total[32:40] * inverse
    new_key = rotated(fresh)
    new_value = pltpu.roll(fresh, 4, 0)
    empty = jnp.zeros((HD - 8, HD), f32)
    new_key = jnp.concatenate([new_key, empty], axis=0).astype(bf16)
    new_value = jnp.concatenate([new_value, empty], axis=0).astype(bf16)

    keys = in_ref[:, 0:LOCAL, :].reshape(CONTEXT, HD)
    values = in_ref[:, LOCAL : 2 * LOCAL, :].reshape(CONTEXT, HD)
    scale = 1.0 / np.sqrt(np.float32(HD))
    contract = (((1,), (1,)), ((), ()))
    scores = lax.dot_general(query, keys, contract, preferred_element_type=f32) * scale
    recent = lax.dot_general(query, new_key, contract, preferred_element_type=f32) * scale
    live = jnp.broadcast_to(table_ref[0:1, 2 * HD : 2 * HD + CONTEXT], scores.shape)
    scores = jnp.where(live > 0.5, scores, masked_score)
    step = lax.broadcasted_iota(jnp.int32, recent.shape, 0) & 3
    recent = jnp.where(
        lax.broadcasted_iota(jnp.int32, recent.shape, 1) <= step, recent, masked_score
    )
    peak = jnp.maximum(
        jnp.max(scores, axis=-1, keepdims=True), jnp.max(recent, axis=-1, keepdims=True)
    )
    weights = jnp.exp(scores - peak)
    recent_weights = jnp.exp(recent - peak)
    count = jnp.sum(weights, axis=-1, keepdims=True) + jnp.sum(
        recent_weights, axis=-1, keepdims=True
    )
    summed = jnp.dot(weights.astype(bf16), values, preferred_element_type=f32) + jnp.dot(
        recent_weights.astype(bf16), new_value, preferred_element_type=f32
    )
    attention = (summed / count).astype(bf16)
    rows = attention.shape[0]
    for g in range(CHIPS):
        out_ref[g * rows : (g + 1) * rows, :] = attention


def output_kernel(pick_ref, in_ref, other_ref, w_ref, out_ref):
    half = CHIPS * REQ * 8
    picked = jnp.dot(pick_ref[:, :half], in_ref[...], preferred_element_type=f32)
    picked = picked + jnp.dot(pick_ref[:, half:], other_ref[...], preferred_element_type=f32)
    attention = jnp.concatenate([picked[0:ROWS], picked[ROWS : 2 * ROWS]], axis=1).astype(bf16)
    width = out_ref.shape[2]
    for k in range(SEQ):
        columns = slice(k * width, (k + 1) * width)
        out_ref[SEQ_ORDER.index(k)] = jnp.dot(
            attention, w_ref[:, columns], preferred_element_type=f32
        ).astype(bf16)


def gather_kernel(in_ref, out_ref):
    total = in_ref[0].astype(f32)
    for k in range(1, SEQ):
        total = total + in_ref[k].astype(f32)
    for s in range(STEPS):
        out_ref[s] = total[s * REQ : (s + 1) * REQ].astype(bf16)


def body(
    step_inputs,
    norm_gain,
    w_query,
    w_keyval,
    w_out,
    key_cache,
    value_cache,
    ctx_len,
    mig_slot,
    mig_shift,
):
    width = step_inputs.shape[2]
    seq = ("seq_y", "seq_z")
    group = lax.axis_index(("chip", "core")).astype(jnp.int32).reshape(1)
    own = lax.axis_index("seq_z").astype(jnp.int32).reshape(1)

    x = pl.pallas_call(
        spread_kernel,
        in_specs=[anywhere()],
        out_specs=in_vmem(),
        out_shape=jax.ShapeDtypeStruct((GROUPS, ROWS, width), bf16),
        scratch_shapes=[pltpu.VMEM(step_inputs.shape, bf16), pltpu.SemaphoreType.DMA],
        compiler_params=params(),
        name="spread",
    )(left(step_inputs))
    order = [[4 * (k ^ (k >> 1)) + low for k in range(4) for low in range(4)]]
    x = lax.all_to_all(x, ("chip", "core"), 0, 0, tiled=True, axis_index_groups=order)
    x = x.reshape(GROUPS * ROWS, width)

    half = np.arange(HD) % (HD // 2)
    freq = jnp.asarray((rope_base ** (-2.0 * half / HD)).astype(np.float32).reshape(1, HD))
    large = (w_query, w_keyval)
    pick_in, pick_out, table, wkv, *split = pl.pallas_call(
        prepare_kernel,
        in_specs=[anywhere()] * 3
        + [pl.BlockSpec(memory_space=pltpu.SMEM)] * 2
        + [anywhere()] * 3,
        out_specs=[in_vmem()] * 6,
        out_shape=[
            pltpu.VMEM((8 * REQ, GROUPS * ROWS), f32),
            pltpu.VMEM((2 * ROWS, GROUPS * REQ * 8), bf16),
            pltpu.VMEM((8, 2 * HD + CONTEXT), f32),
        ]
        + [pltpu.VMEM(w_keyval.shape, bf16)]
        + [pltpu.VMEM((width, PER_KV * HD), bf16)] * 2,
        scratch_shapes=[
            pltpu.SMEM(mig_slot.shape, jnp.int32),
            pltpu.SMEM(mig_shift.shape, jnp.int32),
            pltpu.SMEM(ctx_len.shape, jnp.int32),
            pltpu.VMEM((1, HD), f32),
            pltpu.SemaphoreType.DMA((7,)),
        ],
        compiler_params=params(),
        cost_estimate=pl.CostEstimate(flops=0, bytes_accessed=20_000_000, transcendentals=0),
        name="prepare",
    )(
        left(mig_slot),
        left(mig_shift),
        left(ctx_len),
        group,
        own,
        left(freq),
        *[left(array) for array in large],
    )

    sent = pl.pallas_call(
        project_kernel,
        in_specs=[in_vmem()] * 6 + [anywhere()] * 3,
        out_specs=in_vmem(),
        out_shape=jax.ShapeDtypeStruct((SEQ, CHUNK, HD), bf16),
        scratch_shapes=[pltpu.VMEM((width, PER_KV * HD), bf16)] * 2
        + [pltpu.SemaphoreType.DMA((2,)), pltpu.SemaphoreType.DMA((2 * KVH,))],
        compiler_params=params(),
        name="project",
    )(
        x,
        placed(pick_in),
        norm_gain.reshape(1, width),
        placed(wkv),
        *[placed(part) for part in split],
        left(w_query),
        left(key_cache),
        left(value_cache),
    )
    received = lax.all_to_all(sent, seq, 0, 0, tiled=True)

    attention = pl.pallas_call(
        attend_kernel,
        in_specs=[in_vmem()] * 2,
        out_specs=in_vmem(),
        out_shape=jax.ShapeDtypeStruct((CHIPS * PER_KV * STEPS, HD), bf16),
        compiler_params=params(),
        name="attend",
    )(placed(table), received)
    attention = lax.all_to_all(
        attention.reshape(CHIPS * 4, 8, HD), ("chip", "seq_z"), 0, 0, tiled=True
    ).reshape(CHIPS * 4 * 8, HD)
    other = lax.ppermute(attention, "core", [(0, 1), (1, 0)])

    shares = pl.pallas_call(
        output_kernel,
        in_specs=[in_vmem()] * 4,
        out_specs=in_vmem(),
        out_shape=jax.ShapeDtypeStruct((SEQ, ROWS, width), bf16),
        compiler_params=params(),
        name="output",
    )(placed(pick_out), attention, other, placed(w_out))
    shares = lax.all_to_all(
        shares, seq, 0, 0, tiled=True, axis_index_groups=[SEQ_ORDER]
    )
    return pl.pallas_call(
        gather_kernel,
        in_specs=[in_vmem()],
        out_specs=in_vmem(),
        out_shape=jax.ShapeDtypeStruct((STEPS, REQ, width), bf16),
        compiler_params=params(),
        name="gather",
    )(shares)


def solution(mesh):
    split = Mesh(mesh.devices.reshape(GROUPS // 2, 2, 4, 4), ("chip", "core", "seq_y", "seq_z"))
    seq = ("seq_y", "seq_z")
    group = ("chip", "core")
    specs = (
        P(None, group, seq),
        P(seq),
        P(seq, None),
        P(seq, None),
        P(seq, None),
        P(group, seq, None),
        P(group, seq, None),
        P(group),
        P(),
        P(),
    )
    return jax.shard_map(
        body, mesh=split, in_specs=specs, out_specs=P(None, group, seq), check_vma=False
    )
```
